256 devices in a mesh: dp: 32 (over y, x, core), mp: 8 (over z).
Axes of the slice: x: 4, y: 4, z: 8, core: 2. Of those that a mesh axis runs over, the one named last changes fastest.
Arguments:
- queries: bfloat16 [8192, 2048], P('dp', 'mp'), may hold values from -24 to 24
- context_grad: bfloat16 [8192, 2048], P('dp', 'mp'), may hold values from -6 to 6
- encoder_rows: bfloat16 [28672, 4096], P('dp'), may hold values from -60 to 60
- key_weight: bfloat16 [4096, 2048], P('dp', 'mp'), may hold values from -1 to 1
- value_weight: bfloat16 [4096, 2048], P('dp', 'mp'), may hold values from -0.09375 to 0.09375
- document_lengths: int32 [32, 4], P('dp'), may hold values from 1 to 128, 256 in all within a row
- block_bin: int32 [224], P('dp'), may hold values from 0 to 31, as said below
- block_document: int32 [224], P('dp'), may hold values from 0 to 3
Outputs:
- context: bfloat16 [8192, 2048], P('dp', 'mp')
- query_grad: bfloat16 [8192, 2048], P('dp', 'mp')
- encoder_grad: bfloat16 [28672, 4096], P('dp', 'mp')
- key_weight_grad: bfloat16 [4096, 2048], P('dp', 'mp')
- value_weight_grad: bfloat16 [4096, 2048], P('dp', 'mp')
The draws below stay inside these ranges and needn't reach their ends.
Inputs may be any that keep to these rules, and one draw needn't show every extreme that they name: `block_bin`: each index of dp holds 7 encoder blocks and sends them to 7 different bins; one bin receives a block from every index of dp.
All inputs are finite; a program needn't handle non-finite values.
Results may differ from the reference program's by a relative error of at most 0.03.
The reference program's roundings to bfloat16 on the way count: a program that leaves them out, or rounds other values in their place, can miss the bound.
Values may be sent and summed in bfloat16 or wider, within the bound.
No kernel may reach another device: no remote copies, remote signals or barrier semaphores. Data moves between devices by JAX's collectives and lax.ppermute only.
A program may use at most 128 MiB of HBM per device.

```python
import math
import jax
import jax.numpy as jnp
import numpy as np
from jax import lax

D = 4096
HD = 256
H = 8
BLK = 128
NDOC = 4
EBLK = 7
DEC_DEV = 256
ENC_DEV = 896
TOKENS = 8192
ENC_ROWS = 28672
NBLK = 224
N_DP = 32


def draw_queries(key, part):
    values = jnp.clip(jax.random.normal(jax.random.fold_in(key, 11), (TOKENS, H * HD), jnp.float32), -6.0, 6.0)
    return values.astype(jnp.bfloat16)


def draw_encoder_rows(key, part):
    bin_count = ENC_ROWS // ENC_DEV
    slice_width = D // bin_count
    pairing = jax.random.permutation(jax.random.fold_in(key, 21), bin_count)
    owner = jnp.arange(ENC_ROWS, dtype=jnp.int32) // ENC_DEV
    feature_block = jnp.arange(D, dtype=jnp.int32) // slice_width
    boost = jnp.where(pairing[owner][:, None] == feature_block[None, :], 3.0, 1.0)
    values = jax.random.normal(jax.random.fold_in(key, 24), (ENC_ROWS, D), jnp.float32)
    return jnp.clip(values * boost, -60.0, 60.0).astype(jnp.bfloat16)


def draw_key_weight(key, part):
    noise = jax.random.normal(jax.random.fold_in(key, 31), (D, H * HD), jnp.float32) * D ** (-0.5)
    values = noise
    return jnp.clip(values, -1.0, 1.0).astype(jnp.bfloat16)


def draw_block_bin(key, part):
    bin_count = NBLK // EBLK
    heavy = jax.random.randint(jax.random.fold_in(key, 41), (), 0, bin_count)
    leaning = jax.random.randint(jax.random.fold_in(key, 42), (bin_count,), 0, 4)
    jitter = jax.random.randint(jax.random.fold_in(key, 43), (bin_count, bin_count), 0, 1024)
    columns = jnp.arange(bin_count, dtype=jnp.int32)
    ranking = leaning[None, :] * 2 ** 20 + jitter * 64 + columns[None, :]
    ranking = jnp.where(columns[None, :] == heavy, 2 ** 29, ranking).astype(jnp.int32)
    _, chosen = lax.top_k(ranking, EBLK)
    shuffle_keys = jax.random.randint(jax.random.fold_in(key, 44), (bin_count, EBLK), 0, 1024) * 64 + jnp.arange(EBLK, dtype=jnp.int32)[None, :]
    order = jnp.argsort(shuffle_keys, axis=1)
    chosen = jnp.take_along_axis(chosen, order, axis=1)
    return chosen.reshape(-1).astype(jnp.int32)


def with_ends(values, key, least, top_value):
    place = [jax.random.randint(jax.random.fold_in(key, axis), (), 0, length) for axis, length in enumerate(values.shape)]
    widest = values.shape.index(max(values.shape))
    beside = place[:widest] + [(place[widest] + 1) % values.shape[widest]] + place[widest + 1:]
    return values.at[tuple(place)].set(least).at[tuple(beside)].set(top_value)


def block_scale(stream_key, shape, pieces, least, largest):
    level = 1.0
    for position, parts in pieces:
        steps = jax.random.uniform(jax.random.fold_in(jax.random.fold_in(stream_key, 6), position), (parts,), jnp.float32, least / len(pieces), largest / len(pieces))
        level = level * jnp.repeat(jnp.exp(steps), shape[position] // parts).reshape((-1,) + (1,) * (len(shape) - 1 - position))
    return level


def split_up(count, total, most, skew):
    loads = [(1 << 20) // math.isqrt(rank ** skew) + 1 for rank in range(2, count + 1)]
    spare, holding = total - most - (count - 1), [1] * (count - 1)
    while spare > 0:
        candidates = [i for i in range(count - 1) if holding[i] < most]
        pool, remaining = sum([loads[i] for i in candidates]), spare
        for i in candidates:
            extra = min(most - holding[i], max(1, remaining * loads[i] // pool), spare)
            holding[i] = holding[i] + extra
            spare = spare - extra
    return np.array([most] + holding)


def uneven(own_key, number_of, total, limit, skew):
    if number_of == 2:
        one = jax.random.randint(own_key, (), max(1, total - limit), min(limit, total - 1) + 1)
        return jnp.stack([one, total - one])
    lengths = jnp.asarray(split_up(number_of, total, limit, skew), jnp.int32)
    couples = (number_of - 1) // 2
    source_of, taker = lengths[1:1 + 2 * couples:2], lengths[2:2 + 2 * couples:2]
    margin = jnp.minimum(source_of - 1, limit - taker)
    shifted = jax.random.randint(jax.random.fold_in(own_key, 1), (couples,), 0, 1 << 20) % (margin + 1)
    lengths = lengths.at[1:1 + 2 * couples:2].set(source_of - shifted).at[2:2 + 2 * couples:2].set(taker + shifted)
    return lengths[jax.random.permutation(jax.random.fold_in(own_key, 2), number_of)]


def normal_values(key, shape, spread, limit, shards=(), kind=jnp.bfloat16):
    loudness = block_scale(key, shape, shards, -0.22, 0.18) if shards else 1.0
    result = jax.random.normal(key, shape, jnp.float32) * spread * loudness
    return jnp.minimum(jnp.maximum(result, -limit), limit).astype(kind)


def setup_inputs(seed: int = 0) -> dict:
    key_list = jax.random.split(jax.random.key(seed), 9)
    return {
        "queries": draw_queries(jax.random.fold_in(key_list[8], 71), 0),
        "context_grad": normal_values(key_list[1], (TOKENS, H * HD), 1.0, 6.0, ((0, 32), (1, 8))),
        "encoder_rows": draw_encoder_rows(jax.random.fold_in(key_list[8], 71), 0),
        "key_weight": draw_key_weight(jax.random.fold_in(key_list[8], 71), 0),
        "value_weight": normal_values(key_list[4], (D, H * HD), D ** -0.5, 0.09375, ((0, 32), (1, 8))),
        "document_lengths": jax.vmap(lambda own: uneven(own, NDOC, DEC_DEV, DEC_DEV // 2, 2))(jax.random.split(key_list[5], N_DP)).reshape((N_DP, NDOC)).astype(jnp.int32),
        "block_bin": draw_block_bin(jax.random.fold_in(key_list[8], 71), 0),
        "block_document": with_ends(jax.random.randint(key_list[7], (NBLK,), 0, NDOC), jax.random.fold_in(key_list[7], 1), 0, NDOC - 1).astype(jnp.int32),
    }


masked_value = -1e30


def attend_weights(scores, live_mask):
    present = jnp.any(live_mask, axis=1)[None, :, None]
    blocked = jnp.where(live_mask[None], scores, masked_value)
    highest = jnp.max(blocked, axis=2, keepdims=True)
    highest = jnp.where(present, highest, 0.0)
    raised = jnp.exp(jnp.where(live_mask[None], scores - highest, masked_value))
    totals = jnp.maximum(jnp.sum(raised, axis=2, keepdims=True), 1.0)
    return raised / totals


def reference(queries, context_grad, encoder_rows, key_weight, value_weight, document_lengths, block_bin, block_document):
    width = H * HD
    scaling = HD ** -0.5
    both_weights = jnp.concatenate([key_weight, value_weight], axis=1).astype(jnp.float32)
    key_values = jnp.dot(encoder_rows.astype(jnp.float32), both_weights).astype(jnp.bfloat16)
    kv_blocks = key_values.reshape(N_DP, EBLK, BLK, 2 * width)
    bins_of = block_bin.reshape(N_DP, EBLK)
    docs_of = block_document.reshape(N_DP, EBLK)
    sources = jnp.arange(N_DP, dtype=jnp.int32)
    local_slots = jnp.arange(EBLK, dtype=jnp.int32)
    positions = jnp.arange(DEC_DEV, dtype=jnp.int32)

    def bin_step(grad_blocks, bin_index):
        arrives = bins_of == bin_index
        present = jnp.any(arrives, axis=1)
        local_index = jnp.sum(jnp.where(arrives, local_slots[None, :], 0), axis=1).astype(jnp.int32)
        slot_kv = kv_blocks[sources, local_index]
        slot_doc = jnp.where(present, docs_of[sources, local_index], -1)
        doc_ends = jnp.cumsum(document_lengths[bin_index])
        token_doc = jnp.sum((doc_ends[None, :] <= positions[:, None]).astype(jnp.int32), axis=1)
        live_mask = token_doc[:, None] == jnp.repeat(slot_doc, BLK)[None, :]
        key_rows = slot_kv[:, :, :width].reshape(N_DP * BLK, H, HD).astype(jnp.float32)
        value_rows = slot_kv[:, :, width:].reshape(N_DP * BLK, H, HD).astype(jnp.float32)
        row_start = (bin_index * DEC_DEV).astype(jnp.int32)
        query_rows = lax.dynamic_slice_in_dim(queries, row_start, DEC_DEV, 0).reshape(DEC_DEV, H, HD).astype(jnp.float32)
        grad_rows = lax.dynamic_slice_in_dim(context_grad, row_start, DEC_DEV, 0).reshape(DEC_DEV, H, HD).astype(jnp.float32)
        scores = jnp.einsum("thd,shd->hts", query_rows, key_rows) * scaling
        attention = attend_weights(scores, live_mask)
        rounded = lax.optimization_barrier(attention.astype(jnp.bfloat16)).astype(jnp.float32)
        context = jnp.einsum("hts,shd->thd", rounded, value_rows).astype(jnp.bfloat16)
        grad_raw = jnp.einsum("thd,shd->hts", grad_rows, value_rows)
        deltas = jnp.sum(attention * grad_raw, axis=2, keepdims=True)
        score_grad = lax.optimization_barrier((attention * (grad_raw - deltas) * scaling).astype(jnp.bfloat16)).astype(jnp.float32)
        query_grad = jnp.einsum("hts,shd->thd", score_grad, key_rows).astype(jnp.bfloat16)
        key_grad = jnp.einsum("hts,thd->shd", score_grad, query_rows).astype(jnp.bfloat16)
        value_grad = jnp.einsum("hts,thd->shd", rounded, grad_rows).astype(jnp.bfloat16)
        slot_grads = jnp.concatenate([key_grad.reshape(N_DP, BLK, width), value_grad.reshape(N_DP, BLK, width)], axis=2)
        grad_blocks = jnp.where(arrives[:, :, None, None], slot_grads[:, None], grad_blocks)
        return grad_blocks, (context.reshape(DEC_DEV, width), query_grad.reshape(DEC_DEV, width))

    start_blocks = jnp.zeros((N_DP, EBLK, BLK, 2 * width), jnp.bfloat16)
    grad_blocks, (context_all, query_all) = lax.scan(bin_step, start_blocks, jnp.arange(N_DP, dtype=jnp.int32))
    context = context_all.reshape(TOKENS, width)
    query_grad = query_all.reshape(TOKENS, width)
    kv_grad = grad_blocks.reshape(N_DP, ENC_DEV, 2 * width)
    encoder_split = encoder_rows.reshape(N_DP, ENC_DEV, D)

    def add_source(weight_sum, source):
        partial_value = jnp.dot(encoder_split[source].astype(jnp.float32).T, kv_grad[source].astype(jnp.float32))
        partial_value = lax.optimization_barrier(partial_value.astype(jnp.bfloat16)).astype(jnp.float32)
        return weight_sum + partial_value, None

    weight_sum, _ = lax.scan(add_source, jnp.zeros((D, 2 * width), jnp.float32), jnp.arange(N_DP, dtype=jnp.int32))
    key_weight_grad = weight_sum[:, :width].astype(jnp.bfloat16)
    value_weight_grad = weight_sum[:, width:].astype(jnp.bfloat16)
    encoder_grad = jnp.dot(kv_grad.reshape(ENC_ROWS, 2 * width).astype(jnp.float32), both_weights.T).astype(jnp.bfloat16)
    return (context, query_grad, encoder_grad, key_weight_grad, value_weight_grad)
```

```python
import jax
import jax.numpy as jnp
from jax import lax
from jax.sharding import PartitionSpec as P

HD = 256
BLK = 128


masked_value = -1e30


def attend_weights(scores, live_mask):
    present = jnp.any(live_mask, axis=1)[None, :, None]
    blocked = jnp.where(live_mask[None], scores, masked_value)
    highest = jnp.max(blocked, axis=2, keepdims=True)
    highest = jnp.where(present, highest, 0.0)
    raised = jnp.exp(jnp.where(live_mask[None], scores - highest, masked_value))
    totals = jnp.maximum(jnp.sum(raised, axis=2, keepdims=True), 1.0)
    return raised / totals


def token_documents(lengths, token_count):
    order = jnp.arange(lengths.shape[0], dtype=jnp.int32)
    doc_ends = jnp.sum(jnp.where(order[None, :] <= order[:, None], lengths[None, :], 0), axis=1)
    positions = jnp.arange(token_count, dtype=jnp.int32)
    return jnp.sum((doc_ends[None, :] <= positions[:, None]).astype(jnp.int32), axis=1)


def per_device(
    queries,
    context_grad,
    encoder_rows,
    key_weight,
    value_weight,
    document_lengths,
    block_bin,
    block_document,
):
    bin_count = lax.axis_size("dp")
    full_key, full_value = (
        lax.all_gather(key_weight, "dp", axis=0, tiled=True),
        lax.all_gather(value_weight, "dp", axis=0, tiled=True),
    )
    head_width = full_key.shape[1]
    head_count = head_width // HD
    block_rows = BLK
    blocks_here = block_bin.shape[0]
    both_weights = jnp.concatenate([full_key, full_value], axis=1)
    projected = jnp.dot(encoder_rows, both_weights, preferred_element_type=jnp.float32).astype(
        jnp.bfloat16
    )
    route_table = (block_bin[:, None] == jnp.arange(bin_count, dtype=jnp.int32)[None, :]).astype(
        jnp.bfloat16
    )
    flat_blocks = projected.reshape(blocks_here, block_rows * 2 * head_width)
    outbound = lax.dot_general(
        route_table, flat_blocks, (((0,), (0,)), ((), ())), preferred_element_type=jnp.float32
    )
    outbound = outbound.astype(jnp.bfloat16).reshape(bin_count, block_rows, 2 * head_width)
    slot_docs = (
        lax.dot_general(
            route_table.astype(jnp.float32),
            (block_document + 1).astype(jnp.float32),
            (((0,), (0,)), ((), ())),
        )
        - 1.0
    )
    tag_rows = jnp.broadcast_to(slot_docs[:, None], (bin_count, block_rows)).astype(jnp.bfloat16)
    arrived, arrived_tags = (
        lax.all_to_all(outbound, "dp", split_axis=0, concat_axis=0, tiled=True),
        lax.all_to_all(tag_rows, "dp", split_axis=0, concat_axis=0, tiled=True),
    )
    key_slots = arrived[:, :, :head_width].reshape(bin_count * block_rows, head_count, HD)
    value_slots = arrived[:, :, head_width:].reshape(bin_count * block_rows, head_count, HD)
    token_count = queries.shape[0]
    token_docs = token_documents(document_lengths[0], token_count).astype(jnp.float32)
    live_mask = arrived_tags.reshape(-1).astype(jnp.float32)[None, :] == token_docs[:, None]
    query_heads = queries.reshape(token_count, head_count, HD)
    grad_heads = context_grad.reshape(token_count, head_count, HD)
    scaling = HD ** (-0.5)
    scores = (
        jnp.einsum("thd,shd->hts", query_heads, key_slots, preferred_element_type=jnp.float32)
        * scaling
    )
    attention = attend_weights(scores, live_mask)
    rounded = attention.astype(jnp.bfloat16)
    context = jnp.einsum(
        "hts,shd->thd", rounded, value_slots, preferred_element_type=jnp.float32
    ).astype(jnp.bfloat16)
    grad_raw = jnp.einsum(
        "thd,shd->hts", grad_heads, value_slots, preferred_element_type=jnp.float32
    )
    deltas = jnp.sum(attention * grad_raw, axis=2, keepdims=True)
    score_grad = (attention * (grad_raw - deltas) * scaling).astype(jnp.bfloat16)
    query_grad = jnp.einsum(
        "hts,shd->thd", score_grad, key_slots, preferred_element_type=jnp.float32
    ).astype(jnp.bfloat16)
    key_grad = jnp.einsum(
        "hts,thd->shd", score_grad, query_heads, preferred_element_type=jnp.float32
    ).astype(jnp.bfloat16)
    value_grad = jnp.einsum(
        "hts,thd->shd", rounded, grad_heads, preferred_element_type=jnp.float32
    ).astype(jnp.bfloat16)
    slot_grads = jnp.concatenate(
        [
            key_grad.reshape(bin_count, block_rows, head_width),
            value_grad.reshape(bin_count, block_rows, head_width),
        ],
        axis=2,
    )
    returned = lax.all_to_all(slot_grads, "dp", split_axis=0, concat_axis=0, tiled=True)
    own_grads = jnp.dot(
        route_table,
        returned.reshape(bin_count, block_rows * 2 * head_width),
        preferred_element_type=jnp.float32,
    )
    own_grads = own_grads.astype(jnp.bfloat16).reshape(encoder_rows.shape[0], 2 * head_width)
    weight_terms = lax.dot_general(
        encoder_rows, own_grads, (((0,), (0,)), ((), ())), preferred_element_type=jnp.float32
    )
    weight_sums = lax.psum_scatter(
        weight_terms.astype(jnp.bfloat16), "dp", scatter_dimension=0, tiled=True
    ).astype(jnp.float32)
    key_weight_grad = weight_sums[:, :head_width].astype(jnp.bfloat16)
    value_weight_grad = weight_sums[:, head_width:].astype(jnp.bfloat16)
    row_terms = lax.dot_general(
        own_grads, both_weights, (((1,), (1,)), ((), ())), preferred_element_type=jnp.float32
    )
    encoder_grad = lax.psum_scatter(
        row_terms.astype(jnp.bfloat16), "mp", scatter_dimension=1, tiled=True
    )
    return (
        context.reshape(token_count, head_width),
        query_grad.reshape(token_count, head_width),
        encoder_grad,
        key_weight_grad,
        value_weight_grad,
    )


def solution(mesh):
    in_specs = (
        P("dp", "mp"),
        P("dp", "mp"),
        P("dp", None),
        P("dp", "mp"),
        P("dp", "mp"),
        P("dp", None),
        P("dp"),
        P("dp"),
    )
    out_specs = (P("dp", "mp"), P("dp", "mp"), P("dp", "mp"), P("dp", "mp"), P("dp", "mp"))
    return jax.shard_map(
        per_device, mesh=mesh, in_specs=in_specs, out_specs=out_specs, check_vma=False
    )
```

```python
import functools

import jax
import jax.numpy as jnp
from jax import lax
from jax.experimental import pallas as pl
from jax.experimental.pallas import tpu as pltpu
from jax.sharding import Mesh
from jax.sharding import PartitionSpec as P

HD = 256
BLK = 128
EBLK = 7
NDOC = 4
MASKED = -1e30
SCALE = HD ** (-0.5)
PLANE = ("y", "x")
DP = ("y", "x", "c")
bf16, f32 = jnp.bfloat16, jnp.float32
VMEM = pl.BlockSpec(memory_space=pltpu.VMEM)
SMEM = pl.BlockSpec(memory_space=pltpu.SMEM)
ANY = pl.BlockSpec(memory_space=pl.ANY)


def mul(a, b, da, db):
    return lax.dot_general(a, b, (((da,), (db,)), ((), ())), preferred_element_type=f32)


def params(**more):
    return pltpu.CompilerParams(vmem_limit_bytes=56 * 2**20, **more)


def token_range(b, bins, docs, lengths):
    j, k = bins[b], docs[b]
    first = jnp.int32(0)
    for i in range(NDOC - 1):
        first = first + jnp.where(i < k, lengths[j, i], 0)
    return first, first + lengths[j, k]


def block_scores(b, bins, docs, lengths, kv, qc):
    first, last = token_range(b, bins, docs, lengths)
    key, value = kv[b * BLK : (b + 1) * BLK, :HD], kv[b * BLK : (b + 1) * BLK, HD:]
    scores = mul(key, qc[b, :, :HD], 1, 1) * SCALE
    raw = mul(value, qc[b, :, HD:], 1, 1)
    token = lax.broadcasted_iota(jnp.int32, scores.shape, 1)
    return scores, raw, (token >= first) & (token < last)


def project_kernel(bins, docs, lengths, e, w, tokens, kv, qc, stats, acc, sems):
    step = pl.program_id(0)

    def fetch(b):
        return pltpu.make_async_copy(tokens.at[bins[b], 128:384, :], qc.at[b], sems.at[b])

    @pl.when(step == 0)
    def _():
        for b in range(EBLK):
            fetch(b).start()

    part = jnp.dot(e[...], w[...].reshape(-1, 2 * HD), preferred_element_type=f32)

    @pl.when(step == 0)
    def _():
        acc[...] = part

    @pl.when(step > 0)
    def _():
        acc[...] += part

    @pl.when(step == pl.num_programs(0) - 1)
    def _():
        kv[...] = acc[...].astype(bf16)
        stats[...] = jnp.zeros_like(stats)
        stats[7:8, :] = jnp.full((1, HD), MASKED, f32)
        stats[31:32, :] = jnp.full((1, HD), -1.0, f32)
        for b in range(EBLK):
            fetch(b).wait()
        for b in range(EBLK):
            scores, raw, live = block_scores(b, bins, docs, lengths, kv, qc)
            scores = jnp.where(live, scores, MASKED)
            top = jnp.max(scores, axis=0, keepdims=True)
            raised = jnp.where(live, jnp.exp(scores - top), 0.0)
            stats[b : b + 1, :] = top
            stats[8 + b : 9 + b, :] = jnp.sum(raised, axis=0, keepdims=True)
            stats[16 + b : 17 + b, :] = jnp.sum(raised * raw, axis=0, keepdims=True)
            stats[24 + b : 25 + b, :] = jnp.full((1, HD), bins[b].astype(f32))


def attend_kernel(bins, docs, lengths, kv, qc, stats, grads, grads_t, mine, other):
    core = lax.axis_index("c")
    mine[...] = jnp.zeros_like(mine)
    other[...] = jnp.zeros_like(other)
    tops = stats[:, 0:8, :].reshape(-1, HD)
    sums = stats[:, 8:16, :].reshape(-1, HD)
    dots = stats[:, 16:24, :].reshape(-1, HD)
    owners = stats[:, 24:32, :].reshape(-1, HD)
    for b in range(EBLK):
        scores, raw, live = block_scores(b, bins, docs, lengths, kv, qc)
        same = owners == bins[b].astype(f32)
        masked = jnp.where(same, tops, MASKED)
        top = jnp.max(masked, axis=0, keepdims=True)
        level = jnp.where(same, jnp.exp(masked - top), 0.0)
        total = jnp.maximum(jnp.sum(level * sums, axis=0, keepdims=True), 1.0)
        delta = jnp.sum(level * dots, axis=0, keepdims=True) / total
        attention = jnp.exp(jnp.where(live, scores - top, MASKED)) / total
        rounded = attention.astype(bf16)
        score_grad = (attention * (raw - delta) * SCALE).astype(bf16)
        rows = slice(b * BLK, (b + 1) * BLK)
        query, cotangent = qc[b, :, :HD], qc[b, :, HD:]
        grads[rows, :HD] = mul(score_grad, query, 1, 0).astype(bf16)
        grads[rows, HD:] = mul(rounded, cotangent, 1, 0).astype(bf16)
        grads_t[:HD, rows] = mul(query, score_grad, 0, 1).astype(bf16)
        grads_t[HD:, rows] = mul(cotangent, rounded, 0, 1).astype(bf16)
        context = mul(rounded, kv[rows, HD:], 0, 0).astype(bf16)
        query_grad = mul(score_grad, kv[rows, :HD], 0, 0).astype(bf16)
        slot = bins[b] // 2
        here = bins[b] % 2 == core

        @pl.when(here)
        def _():
            mine[slot, :, :HD] = context
            mine[slot, :, HD:] = query_grad

        @pl.when(jnp.logical_not(here))
        def _():
            other[slot, :, :HD] = context
            other[slot, :, HD:] = query_grad


def rows_kernel(grads, w, out):
    out[0] = mul(grads[...], w[...].reshape(-1, 2 * HD), 1, 1).astype(bf16)


def weights_kernel(grads_t, e, mine, other):
    core = lax.axis_index("c")
    term = jnp.dot(grads_t[...], e[...], preferred_element_type=f32).astype(bf16)
    for i in range(term.shape[1] // 256):
        even, odd = term[:, i * 256 : i * 256 + 128], term[:, i * 256 + 128 : i * 256 + 256]
        mine[i] = jnp.where(core == 0, even, odd)
        other[i] = jnp.where(core == 0, odd, even)


def shape(*dims, dtype=bf16):
    return jax.ShapeDtypeStruct(dims, dtype)


def per_device(queries, context_grad, encoder_rows, key_weight, value_weight, document_lengths, block_bin, block_document):
    rows, width = encoder_rows.shape
    tokens = queries.shape[0]
    bin_count = 32
    packed = jnp.concatenate(
        [
            jnp.concatenate([key_weight, value_weight], axis=1),
            jnp.concatenate([queries, context_grad], axis=1),
            jnp.pad(document_lengths.astype(bf16), ((0, 15), (0, 2 * HD - NDOC))),
        ],
        axis=0,
    )
    gathered = lax.all_gather(packed, DP, axis=0, tiled=False)
    lengths = gathered[:, 384, :NDOC].astype(jnp.int32)

    kv, qc, stats = pl.pallas_call(
        project_kernel,
        grid=(8,),
        in_specs=[
            SMEM,
            SMEM,
            SMEM,
            pl.BlockSpec((rows, 512), lambda k: (0, k)),
            pl.BlockSpec((4, 128, 2 * HD), lambda k: (k, 0, 0)),
            ANY,
        ],
        out_specs=[
            pl.BlockSpec((rows, 2 * HD), lambda k: (0, 0)),
            pl.BlockSpec((EBLK, tokens, 2 * HD), lambda k: (0, 0, 0)),
            pl.BlockSpec((32, HD), lambda k: (0, 0)),
        ],
        out_shape=[shape(rows, 2 * HD), shape(EBLK, tokens, 2 * HD), shape(32, HD, dtype=f32)],
        scratch_shapes=[pltpu.VMEM((rows, 2 * HD), f32), pltpu.SemaphoreType.DMA((EBLK,))],
        compiler_params=params(),
        name="project",
    )(block_bin, block_document, lengths, encoder_rows, gathered, gathered)

    all_stats = lax.all_to_all(
        jnp.broadcast_to(stats[None], (bin_count, 32, HD)), DP, split_axis=0, concat_axis=0, tiled=True
    )

    grads, grads_t, mine, other = pl.pallas_call(
        attend_kernel,
        in_specs=[SMEM, SMEM, SMEM, VMEM, VMEM, VMEM],
        out_specs=[VMEM] * 4,
        out_shape=[
            shape(rows, 2 * HD),
            shape(2 * HD, rows),
            shape(16, tokens, 2 * HD),
            shape(16, tokens, 2 * HD),
        ],
        compiler_params=params(),
        name="attend",
    )(block_bin, block_document, lengths, kv, qc, all_stats)

    def swap(v):
        return lax.ppermute(v, "c", [(0, 1), (1, 0)])

    def spread(own, arrived):
        both = (own.astype(f32) + arrived.astype(f32)).astype(bf16)
        return lax.all_to_all(both, PLANE, split_axis=0, concat_axis=0, tiled=True)

    row_terms = pl.pallas_call(
        rows_kernel,
        grid=(8,),
        in_specs=[
            pl.BlockSpec((rows, 2 * HD), lambda k: (0, 0)),
            pl.BlockSpec((4, 128, 2 * HD), lambda k: (k, 0, 0)),
        ],
        out_specs=pl.BlockSpec((1, rows, 512), lambda k: (k, 0, 0)),
        out_shape=shape(8, rows, 512),
        compiler_params=params(),
        name="row_terms",
    )(grads, gathered)
    encoder_grad = lax.psum_scatter(row_terms, "mp", scatter_dimension=0, tiled=False)

    token_sums = spread(mine, swap(other))

    mine_w, other_w = pl.pallas_call(
        weights_kernel,
        grid=(8,),
        in_specs=[
            pl.BlockSpec((2 * HD, rows), lambda k: (0, 0)),
            pl.BlockSpec((rows, 512), lambda k: (0, k)),
        ],
        out_specs=[pl.BlockSpec((2, 2 * HD, 128), lambda k: (k, 0, 0))] * 2,
        out_shape=[shape(16, 2 * HD, 128)] * 2,
        compiler_params=params(),
        name="weight_terms",
    )(grads_t, encoder_rows)
    weight_sums = spread(mine_w, swap(other_w))

    outs = jnp.sum(token_sums.astype(f32), axis=0).astype(bf16)
    weights = jnp.sum(weight_sums.astype(f32), axis=0).astype(bf16).T
    return outs[:, :HD], outs[:, HD:], encoder_grad, weights[:, :HD], weights[:, HD:]


def solution(mesh):
    fine = Mesh(mesh.devices.reshape(4, 4, 2, 8), ("y", "x", "c", "mp"))
    both, first = P(DP, "mp"), P(DP)
    return jax.shard_map(
        per_device,
        mesh=fine,
        in_specs=(both, both, P(DP, None), both, both, P(DP, None), first, first),
        out_specs=(both,) * 5,
        check_vma=False,
    )
```

```python
import jax
import jax.numpy as jnp
from jax import lax
from jax.experimental import pallas as pl
from jax.experimental.pallas import tpu as pltpu
from jax.sharding import Mesh
from jax.sharding import PartitionSpec as P

HD = 256
BLK = 128
EBLK = 7
NDOC = 4
WIN = 128
BINS = 32
MASKED = -1e30
SCALE = HD ** (-0.5)
PLANE = ("y", "x")
DP = ("y", "x", "c")
bf16, f32 = jnp.bfloat16, jnp.float32
VMEM = pl.BlockSpec(memory_space=pltpu.VMEM)
SMEM = pl.BlockSpec(memory_space=pltpu.SMEM)
COST = pl.CostEstimate(flops=3758096384, bytes_accessed=16 * 2**20, transcendentals=0)
ANY = pl.BlockSpec(memory_space=pl.ANY)


def mul(a, b, da, db):
    return lax.dot_general(a, b, (((da,), (db,)), ((), ())), preferred_element_type=f32)


def params(**more):
    return pltpu.CompilerParams(vmem_limit_bytes=56 * 2**20, **more)


def token_range(b, bins, docs, lengths):
    j, k = bins[b], docs[b]
    first = jnp.int32(0)
    for i in range(NDOC - 1):
        first = first + jnp.where(i < k, lengths[j, i], 0)
    return first, first + lengths[j, k]


def to_window(row, first):
    return pltpu.roll(row, 2 * WIN - first, 1)[:, :WIN]


def from_window(row, first):
    return pltpu.roll(jnp.concatenate([row, jnp.zeros_like(row)], axis=1), first, 1)


def block_scores(b, bins, docs, lengths, kv, qc):
    first, last = token_range(b, bins, docs, lengths)
    key, value = kv[b * BLK : (b + 1) * BLK, :HD], kv[b * BLK : (b + 1) * BLK, HD:]
    scores = mul(key, qc[b, :, :HD], 1, 1) * SCALE
    raw = mul(value, qc[b, :, HD:], 1, 1)
    token = lax.broadcasted_iota(jnp.int32, scores.shape, 1)
    return scores, raw, (token >= first) & (token < last), first


def project_kernel(bins, docs, lengths, e, w, tokens, kv, qc, stats, acc, sems):
    step = pl.program_id(0)

    def fetch(b):
        return pltpu.make_async_copy(tokens.at[bins[b], 128:384, :], qc.at[b], sems.at[b])

    @pl.when(step == 0)
    def _():
        for b in range(EBLK):
            fetch(b).start()

    part = jnp.dot(e[...], w[...].reshape(-1, 2 * HD), preferred_element_type=f32)

    @pl.when(step == 0)
    def _():
        acc[...] = part

    @pl.when(step > 0)
    def _():
        acc[...] += part

    @pl.when(step == pl.num_programs(0) - 1)
    def _():
        kv[...] = acc[...].astype(bf16)
        stats[...] = jnp.zeros_like(stats)
        for b in range(EBLK):
            fetch(b).wait()
        for b in range(EBLK):
            scores, raw, live, first = block_scores(b, bins, docs, lengths, kv, qc)
            scores = jnp.where(live, scores, MASKED)
            top = jnp.max(scores, axis=0, keepdims=True)
            raised = jnp.where(live, jnp.exp(scores - top), 0.0)
            stats[b : b + 1, :] = to_window(top, first)
            stats[8 + b : 9 + b, :] = to_window(jnp.sum(raised, axis=0, keepdims=True), first)
            stats[16 + b : 17 + b, :] = to_window(jnp.sum(raised * raw, axis=0, keepdims=True), first)


def attend_kernel(bins, docs, lengths, kv, qc, stats, ids, grads, grads_t, mine, other, zero, made, sems):
    core = lax.axis_index("c")

    def send(source, j, do):
        here = lax.rem(j, 2) == core

        @pl.when(here)
        def _():
            do(pltpu.make_async_copy(source, mine.at[lax.div(j, 2)], sems.at[j]))

        @pl.when(jnp.logical_not(here))
        def _():
            do(pltpu.make_async_copy(source, other.at[lax.div(j, 2)], sems.at[j]))

    zero[...] = jnp.zeros_like(zero)

    def clear(j, carry):
        used = bins[0] == j
        for b in range(1, EBLK):
            used = used | (bins[b] == j)

        @pl.when(jnp.logical_not(used))
        def _():
            send(zero, j, lambda copy: copy.start())

        return carry

    lax.fori_loop(0, BINS, clear, 0)

    tops = stats[:, 0:8, :].reshape(-1, WIN)
    sums = stats[:, 8:16, :].reshape(-1, WIN)
    dots = stats[:, 16:24, :].reshape(-1, WIN)
    owners = ids[...].reshape(-1, WIN)
    for b in range(EBLK):
        scores, raw, live, first = block_scores(b, bins, docs, lengths, kv, qc)
        same = owners == (bins[b] * NDOC + docs[b]).astype(f32)
        masked = jnp.where(same, tops, MASKED)
        top = jnp.max(masked, axis=0, keepdims=True)
        level = jnp.where(same, jnp.exp(masked - top), 0.0)
        total = jnp.maximum(jnp.sum(level * sums, axis=0, keepdims=True), 1.0)
        delta = jnp.sum(level * dots, axis=0, keepdims=True) / total
        top, delta = from_window(top, first), from_window(delta, first)
        total = jnp.maximum(from_window(total, first), 1.0)
        attention = jnp.exp(jnp.where(live, scores - top, MASKED)) / total
        rounded = attention.astype(bf16)
        score_grad = (attention * (raw - delta) * SCALE).astype(bf16)
        rows = slice(b * BLK, (b + 1) * BLK)
        query, cotangent = qc[b, :, :HD], qc[b, :, HD:]
        made[b, :, :HD] = mul(rounded, kv[rows, HD:], 0, 0).astype(bf16)
        made[b, :, HD:] = mul(score_grad, kv[rows, :HD], 0, 0).astype(bf16)
        send(made.at[b], bins[b], lambda copy: copy.start())
        grads[rows, :HD] = mul(score_grad, query, 1, 0).astype(bf16)
        grads[rows, HD:] = mul(rounded, cotangent, 1, 0).astype(bf16)
        grads_t[:HD, rows] = mul(query, score_grad, 0, 1).astype(bf16)
        grads_t[HD:, rows] = mul(cotangent, rounded, 0, 1).astype(bf16)

    def finish(j, carry):
        send(zero, j, lambda copy: copy.wait())
        return carry

    lax.fori_loop(0, BINS, finish, 0)


def rows_kernel(grads, w, out):
    terms = mul(grads[...], w[...].reshape(-1, 2 * HD), 1, 1).astype(bf16)
    for i in range(out.shape[0]):
        out[i] = terms[:, i * 512 : (i + 1) * 512]


def weights_kernel(grads_t, e, mine, other):
    core = lax.axis_index("c")
    term = jnp.dot(grads_t[...], e[...], preferred_element_type=f32).astype(bf16)
    for i in range(term.shape[1] // 256):
        even, odd = term[:, i * 256 : i * 256 + 128], term[:, i * 256 + 128 : i * 256 + 256]
        mine[i] = jnp.where(core == 0, even, odd)
        other[i] = jnp.where(core == 0, odd, even)


def shape(*dims, dtype=bf16):
    return jax.ShapeDtypeStruct(dims, dtype)


def per_device(queries, context_grad, encoder_rows, key_weight, value_weight, document_lengths, block_bin, block_document):
    rows, width = encoder_rows.shape
    tokens = queries.shape[0]
    packed = jnp.concatenate(
        [
            jnp.concatenate([key_weight, value_weight], axis=1),
            jnp.concatenate([queries, context_grad], axis=1),
        ],
        axis=0,
    )
    gathered = lax.all_gather(packed, DP, axis=0, tiled=False)

    def share(v):
        spread_out = jnp.broadcast_to(v[None], (BINS, *v.shape))
        return lax.all_to_all(spread_out, DP, split_axis=0, concat_axis=0, tiled=True)

    facts = jnp.concatenate([document_lengths[0], block_bin * NDOC + block_document, jnp.full((1,), -1, jnp.int32)])
    facts = share(facts[None, :])[:, 0, :]
    lengths = facts[:, :NDOC]
    ids = jnp.broadcast_to(facts[:, NDOC:, None].astype(f32), (BINS, 8, WIN))

    kv, qc, stats = pl.pallas_call(
        project_kernel,
        grid=(4,),
        in_specs=[
            SMEM,
            SMEM,
            SMEM,
            pl.BlockSpec((rows, 1024), lambda k: (0, k)),
            pl.BlockSpec((8, 128, 2 * HD), lambda k: (k, 0, 0)),
            ANY,
        ],
        out_specs=[
            pl.BlockSpec((rows, 2 * HD), lambda k: (0, 0)),
            pl.BlockSpec((EBLK, tokens, 2 * HD), lambda k: (0, 0, 0)),
            pl.BlockSpec((24, WIN), lambda k: (0, 0)),
        ],
        out_shape=[shape(rows, 2 * HD), shape(EBLK, tokens, 2 * HD), shape(24, WIN, dtype=f32)],
        scratch_shapes=[pltpu.VMEM((rows, 2 * HD), f32), pltpu.SemaphoreType.DMA((EBLK,))],
        compiler_params=params(),
        name="project",
    )(block_bin, block_document, lengths, encoder_rows, gathered, gathered)

    all_stats = share(stats)

    grads, grads_t, mine, other = pl.pallas_call(
        attend_kernel,
        in_specs=[SMEM, SMEM, SMEM, VMEM, VMEM, VMEM, VMEM],
        out_specs=[VMEM, VMEM, ANY, ANY],
        out_shape=[
            shape(rows, 2 * HD),
            shape(2 * HD, rows),
            shape(16, tokens, 2 * HD),
            shape(16, tokens, 2 * HD),
        ],
        scratch_shapes=[
            pltpu.VMEM((tokens, 2 * HD), bf16),
            pltpu.VMEM((EBLK, tokens, 2 * HD), bf16),
            pltpu.SemaphoreType.DMA((BINS,)),
        ],
        compiler_params=params(),
        name="attend",
    )(block_bin, block_document, lengths, kv, qc, all_stats, ids)

    def swap(v):
        return lax.ppermute(v, "c", [(0, 1), (1, 0)])

    def spread(v):
        return lax.all_to_all(v, PLANE, split_axis=0, concat_axis=0, tiled=True)

    def add(a, b):
        return (a.astype(f32) + b.astype(f32)).astype(bf16)

    arrived = swap(other)

    row_terms = pl.pallas_call(
        rows_kernel,
        grid=(4,),
        in_specs=[
            pl.BlockSpec((rows, 2 * HD), lambda k: (0, 0)),
            pl.BlockSpec((8, 128, 2 * HD), lambda k: (k, 0, 0)),
        ],
        out_specs=pl.BlockSpec((2, rows, 512), lambda k: (k, 0, 0)),
        out_shape=shape(8, rows, 512),
        compiler_params=params(),
        cost_estimate=COST,
        name="row_terms",
    )(grads, gathered)
    encoder_grad = lax.psum_scatter(row_terms, "mp", scatter_dimension=0, tiled=False)

    pair_sums = add(mine, arrived)
    pair_sums, grads_t = lax.optimization_barrier((pair_sums, grads_t))
    token_sums = spread(pair_sums)

    mine_w, other_w = pl.pallas_call(
        weights_kernel,
        grid=(4,),
        in_specs=[
            pl.BlockSpec((2 * HD, rows), lambda k: (0, 0)),
            pl.BlockSpec((rows, 1024), lambda k: (0, k)),
        ],
        out_specs=[pl.BlockSpec((4, 2 * HD, 128), lambda k: (k, 0, 0))] * 2,
        out_shape=[shape(16, 2 * HD, 128)] * 2,
        compiler_params=params(),
        cost_estimate=COST,
        name="weight_terms",
    )(grads_t, encoder_rows)
    weight_sums = spread(add(mine_w, swap(other_w)))

    outs = jnp.sum(token_sums.astype(f32), axis=0).astype(bf16)
    weights = jnp.sum(weight_sums.astype(f32), axis=0).astype(bf16).T
    return outs[:, :HD], outs[:, HD:], encoder_grad, weights[:, :HD], weights[:, HD:]


def solution(mesh):
    fine = Mesh(mesh.devices.reshape(4, 4, 2, 8), ("y", "x", "c", "mp"))
    both, first = P(DP, "mp"), P(DP)
    return jax.shard_map(
        per_device,
        mesh=fine,
        in_specs=(both, both, P(DP, None), both, both, P(DP, None), first, first),
        out_specs=(both,) * 5,
        check_vma=False,
    )
```

```python
import jax
import jax.numpy as jnp
from jax import lax
from jax.experimental import pallas as pl
from jax.experimental.pallas import tpu as pltpu
from jax.sharding import Mesh
from jax.sharding import PartitionSpec as P

HD = 256
BLK = 128
EBLK = 7
NDOC = 4
WIN = 128
BINS = 32
MASKED = -1e30
SCALE = HD ** (-0.5)
PLANE = ("y", "x")
DP = ("y", "x", "c")
bf16, f32 = jnp.bfloat16, jnp.float32
VMEM = pl.BlockSpec(memory_space=pltpu.VMEM)
SMEM = pl.BlockSpec(memory_space=pltpu.SMEM)
COST = pl.CostEstimate(flops=3758096384, bytes_accessed=16 * 2**20, transcendentals=0)
ANY = pl.BlockSpec(memory_space=pl.ANY)


def mul(a, b, da, db):
    return lax.dot_general(a, b, (((da,), (db,)), ((), ())), preferred_element_type=f32)


def params(**more):
    return pltpu.CompilerParams(vmem_limit_bytes=56 * 2**20, **more)


def token_range(b, bins, docs, lengths):
    j, k = bins[b], docs[b]
    first = jnp.int32(0)
    for i in range(NDOC - 1):
        first = first + jnp.where(i < k, lengths[j, i], 0)
    return first, first + lengths[j, k]


def block_scores(b, bins, docs, lengths, kv, qc):
    first, last = token_range(b, bins, docs, lengths)
    key, value = kv[b * BLK : (b + 1) * BLK, :HD], kv[b * BLK : (b + 1) * BLK, HD:]
    scores = mul(key, qc[b, :, :HD], 1, 1) * SCALE
    raw = mul(value, qc[b, :, HD:], 1, 1)
    return scores, raw, lax.broadcasted_iota(jnp.int32, scores.shape, 1) < last - first


def project_kernel(bins, docs, lengths, e, w, tokens, kv, qc, shared, acc, fetched, stats, sems):
    step = pl.program_id(0)

    def fetch(b):
        return pltpu.make_async_copy(tokens.at[bins[b], 128:384, :], fetched.at[b], sems.at[b])

    @pl.when(step == 0)
    def _():
        for b in range(EBLK):
            fetch(b).start()

    part = jnp.dot(e[...], w[...].reshape(-1, 2 * HD), preferred_element_type=f32)

    @pl.when(step == 0)
    def _():
        acc[...] = part

    @pl.when(step > 0)
    def _():
        acc[...] += part

    @pl.when(step == pl.num_programs(0) - 1)
    def _():
        kv[...] = acc[...].astype(bf16)
        stats[...] = jnp.zeros_like(stats)
        for b in range(EBLK):
            fetch(b).wait()
            first, _ = token_range(b, bins, docs, lengths)
            turned = pltpu.roll(fetched[b].astype(f32), lax.rem(2 * WIN - first, 2 * WIN), 0)
            qc[b] = turned[:WIN].astype(bf16)
        for b in range(EBLK):
            scores, raw, live = block_scores(b, bins, docs, lengths, kv, qc)
            scores = jnp.where(live, scores, MASKED)
            top = jnp.max(scores, axis=0, keepdims=True)
            raised = jnp.where(live, jnp.exp(scores - top), 0.0)
            stats[b : b + 1, :] = top
            stats[8 + b : 9 + b, :] = jnp.sum(raised, axis=0, keepdims=True)
            stats[16 + b : 17 + b, :] = jnp.sum(raised * raw, axis=0, keepdims=True)
        shared[...] = jnp.broadcast_to(stats[...][None], shared.shape)


def attend_kernel(bins, docs, lengths, kv, qc, stats, ids, grads, grads_t, slots, zero, made, sems):
    def copy(source, j):
        return pltpu.make_async_copy(source, slots.at[j], sems.at[j])

    zero[...] = jnp.zeros_like(zero)

    def clear(j, carry):
        used = bins[0] == j
        for b in range(1, EBLK):
            used = used | (bins[b] == j)

        @pl.when(jnp.logical_not(used))
        def _():
            copy(zero, j).start()

        return carry

    lax.fori_loop(0, BINS, clear, 0)

    tops = stats[:, 0:8, :].reshape(-1, WIN)
    sums = stats[:, 8:16, :].reshape(-1, WIN)
    dots = stats[:, 16:24, :].reshape(-1, WIN)
    owners = ids[...].reshape(-1, WIN)
    for b in range(EBLK):
        scores, raw, live = block_scores(b, bins, docs, lengths, kv, qc)
        same = owners == (bins[b] * NDOC + docs[b]).astype(f32)
        masked = jnp.where(same, tops, MASKED)
        top = jnp.max(masked, axis=0, keepdims=True)
        level = jnp.where(same, jnp.exp(masked - top), 0.0)
        total = jnp.maximum(jnp.sum(level * sums, axis=0, keepdims=True), 1.0)
        delta = jnp.sum(level * dots, axis=0, keepdims=True) / total
        attention = jnp.exp(jnp.where(live, scores - top, MASKED)) / total
        rounded = attention.astype(bf16)
        score_grad = (attention * (raw - delta) * SCALE).astype(bf16)
        rows = slice(b * BLK, (b + 1) * BLK)
        query, cotangent = qc[b, :, :HD], qc[b, :, HD:]
        made[b, :, :HD] = mul(rounded, kv[rows, HD:], 0, 0).astype(bf16)
        made[b, :, HD:] = mul(score_grad, kv[rows, :HD], 0, 0).astype(bf16)
        copy(made.at[b], bins[b]).start()
        grads[rows, :HD] = mul(score_grad, query, 1, 0).astype(bf16)
        grads[rows, HD:] = mul(rounded, cotangent, 1, 0).astype(bf16)
        grads_t[:HD, rows] = mul(query, score_grad, 0, 1).astype(bf16)
        grads_t[HD:, rows] = mul(cotangent, rounded, 0, 1).astype(bf16)

    def finish(j, carry):
        copy(zero, j).wait()
        return carry

    lax.fori_loop(0, BINS, finish, 0)


def collect_kernel(docs, lengths, windows, context, query_grad, acc):
    step = pl.program_id(0)

    @pl.when(step == 0)
    def _():
        acc[...] = jnp.zeros_like(acc)

    for i in range(windows.shape[0]):
        acc[docs[step * windows.shape[0] + i]] += windows[i].astype(f32)

    @pl.when(step == pl.num_programs(0) - 1)
    def _():
        total = jnp.concatenate([acc[0], jnp.zeros_like(acc[0])], axis=0)
        first = lengths[0, 0]
        for k in range(1, NDOC):
            total += pltpu.roll(jnp.concatenate([acc[k], jnp.zeros_like(acc[k])], axis=0), first, 0)
            first = first + lengths[0, k]
        context[...] = total[:, :HD].astype(bf16)
        query_grad[...] = total[:, HD:].astype(bf16)


def rows_kernel(grads, w, out):
    terms = mul(grads[...], w[...].reshape(-1, 2 * HD), 1, 1).astype(bf16)
    for i in range(out.shape[0]):
        out[i] = terms[:, i * 512 : (i + 1) * 512]


def weights_kernel(grads_t, e, mine, other):
    core = lax.axis_index("c")
    term = jnp.dot(grads_t[...], e[...], preferred_element_type=f32).astype(bf16)
    for i in range(term.shape[1] // 256):
        even, odd = term[:, i * 256 : i * 256 + 128], term[:, i * 256 + 128 : i * 256 + 256]
        mine[i] = jnp.where(core == 0, even, odd)
        other[i] = jnp.where(core == 0, odd, even)


def shape(*dims, dtype=bf16):
    return jax.ShapeDtypeStruct(dims, dtype)


def per_device(queries, context_grad, encoder_rows, key_weight, value_weight, document_lengths, block_bin, block_document):
    rows, width = encoder_rows.shape
    tokens = queries.shape[0]
    packed = jnp.concatenate(
        [
            jnp.concatenate([key_weight, value_weight], axis=1),
            jnp.concatenate([queries, context_grad], axis=1),
        ],
        axis=0,
    )
    gathered = lax.all_gather(packed, DP, axis=0, tiled=False)

    def share(v):
        spread_out = jnp.broadcast_to(v[None], (BINS, *v.shape))
        return lax.all_to_all(spread_out, DP, split_axis=0, concat_axis=0, tiled=True)

    facts = jnp.concatenate([document_lengths[0], block_bin * NDOC + block_document, jnp.full((1,), -1, jnp.int32)])
    facts = share(facts[None, :])[:, 0, :]
    lengths = facts[:, :NDOC]
    ids = jnp.broadcast_to(facts[:, NDOC:, None].astype(f32), (BINS, 8, WIN))
    sent = facts[:, NDOC : NDOC + EBLK]
    me = lax.axis_index(DP)
    sent_docs = jnp.sum(jnp.where(sent // NDOC == me, sent % NDOC, 0), axis=1)
    ids, sent_docs, lengths, gathered = lax.optimization_barrier((ids, sent_docs, lengths, gathered))

    kv, qc, stats = pl.pallas_call(
        project_kernel,
        grid=(4,),
        in_specs=[
            SMEM,
            SMEM,
            SMEM,
            pl.BlockSpec((rows, 1024), lambda k: (0, k)),
            pl.BlockSpec((8, 128, 2 * HD), lambda k: (k, 0, 0)),
            ANY,
        ],
        out_specs=[
            pl.BlockSpec((rows, 2 * HD), lambda k: (0, 0)),
            pl.BlockSpec((EBLK, WIN, 2 * HD), lambda k: (0, 0, 0)),
            pl.BlockSpec((BINS, 24, WIN), lambda k: (0, 0, 0)),
        ],
        out_shape=[shape(rows, 2 * HD), shape(EBLK, WIN, 2 * HD), shape(BINS, 24, WIN, dtype=f32)],
        scratch_shapes=[
            pltpu.VMEM((rows, 2 * HD), f32),
            pltpu.VMEM((EBLK, tokens, 2 * HD), bf16),
            pltpu.VMEM((24, WIN), f32),
            pltpu.SemaphoreType.DMA((EBLK,)),
        ],
        compiler_params=params(),
        name="project",
    )(block_bin, block_document, lengths, encoder_rows, gathered, gathered)

    all_stats = lax.all_to_all(stats, DP, split_axis=0, concat_axis=0, tiled=True)

    grads, grads_t, slots = pl.pallas_call(
        attend_kernel,
        in_specs=[SMEM, SMEM, SMEM, VMEM, VMEM, VMEM, VMEM],
        out_specs=[VMEM, VMEM, ANY],
        out_shape=[
            shape(rows, 2 * HD),
            shape(2 * HD, rows),
            shape(BINS, WIN, 2 * HD),
        ],
        scratch_shapes=[
            pltpu.VMEM((WIN, 2 * HD), bf16),
            pltpu.VMEM((EBLK, WIN, 2 * HD), bf16),
            pltpu.SemaphoreType.DMA((BINS,)),
        ],
        compiler_params=params(),
        name="attend",
    )(block_bin, block_document, lengths, kv, qc, all_stats, ids)

    windows = lax.all_to_all(slots, DP, split_axis=0, concat_axis=0, tiled=True)

    row_terms = pl.pallas_call(
        rows_kernel,
        grid=(4,),
        in_specs=[
            pl.BlockSpec((rows, 2 * HD), lambda k: (0, 0)),
            pl.BlockSpec((8, 128, 2 * HD), lambda k: (k, 0, 0)),
        ],
        out_specs=pl.BlockSpec((2, rows, 512), lambda k: (k, 0, 0)),
        out_shape=shape(8, rows, 512),
        compiler_params=params(),
        cost_estimate=COST,
        name="row_terms",
    )(grads, gathered)
    encoder_grad = lax.psum_scatter(row_terms, "mp", scatter_dimension=0, tiled=False)


    mine_w, other_w = pl.pallas_call(
        weights_kernel,
        grid=(4,),
        in_specs=[
            pl.BlockSpec((2 * HD, rows), lambda k: (0, 0)),
            pl.BlockSpec((rows, 1024), lambda k: (0, k)),
        ],
        out_specs=[pl.BlockSpec((4, 2 * HD, 128), lambda k: (k, 0, 0))] * 2,
        out_shape=[shape(16, 2 * HD, 128)] * 2,
        compiler_params=params(),
        cost_estimate=COST,
        name="weight_terms",
    )(grads_t, encoder_rows)
    arrived = lax.ppermute(other_w, "c", [(0, 1), (1, 0)])
    pair_sums = (mine_w.astype(f32) + arrived.astype(f32)).astype(bf16)
    windows, pair_sums = lax.optimization_barrier((windows, pair_sums))
    weight_sums = lax.all_to_all(pair_sums, PLANE, split_axis=0, concat_axis=0, tiled=True)

    context, query_grad = pl.pallas_call(
        collect_kernel,
        grid=(8,),
        in_specs=[SMEM, SMEM, pl.BlockSpec((4, WIN, 2 * HD), lambda k: (k, 0, 0))],
        out_specs=[pl.BlockSpec((tokens, HD), lambda k: (0, 0))] * 2,
        out_shape=[shape(tokens, HD)] * 2,
        scratch_shapes=[pltpu.VMEM((NDOC, WIN, 2 * HD), f32)],
        compiler_params=params(),
        name="collect",
    )(sent_docs, document_lengths, windows)

    weights = jnp.sum(weight_sums.astype(f32), axis=0).astype(bf16).T
    return context, query_grad, encoder_grad, weights[:, :HD], weights[:, HD:]


def solution(mesh):
    fine = Mesh(mesh.devices.reshape(4, 4, 2, 8), ("y", "x", "c", "mp"))
    both, first = P(DP, "mp"), P(DP)
    return jax.shard_map(
        per_device,
        mesh=fine,
        in_specs=(both, both, P(DP, None), both, both, P(DP, None), first, first),
        out_specs=(both,) * 5,
        check_vma=False,
    )
```

```python
import jax
import jax.numpy as jnp
from jax import lax
from jax.experimental import pallas as pl
from jax.experimental.pallas import tpu as pltpu
from jax.sharding import Mesh
from jax.sharding import PartitionSpec as P

HD = 256
BLK = 128
EBLK = 7
NDOC = 4
WIN = 128
BINS = 32
MASKED = -1e30
SCALE = HD ** (-0.5)
DP = ("y", "x", "c")
bf16, f32 = jnp.bfloat16, jnp.float32
VMEM = pl.BlockSpec(memory_space=pltpu.VMEM)
SMEM = pl.BlockSpec(memory_space=pltpu.SMEM)
COST = pl.CostEstimate(flops=3758096384, bytes_accessed=16 * 2**20, transcendentals=0)
ANY = pl.BlockSpec(memory_space=pl.ANY)


def mul(a, b, da, db):
    return lax.dot_general(a, b, (((da,), (db,)), ((), ())), preferred_element_type=f32)


def params(**more):
    return pltpu.CompilerParams(vmem_limit_bytes=56 * 2**20, **more)


def token_range(b, bins, docs, lengths):
    j, k = bins[b], docs[b]
    first = jnp.int32(0)
    for i in range(NDOC - 1):
        first = first + jnp.where(i < k, lengths[j, i], 0)
    return first, first + lengths[j, k]


def block_scores(b, bins, docs, lengths, kv, qc):
    first, last = token_range(b, bins, docs, lengths)
    key, value = kv[b * BLK : (b + 1) * BLK, :HD], kv[b * BLK : (b + 1) * BLK, HD:]
    scores = mul(key, qc[b, :, :HD], 1, 1) * SCALE
    raw = mul(value, qc[b, :, HD:], 1, 1)
    return scores, raw, lax.broadcasted_iota(jnp.int32, scores.shape, 1) < last - first


def project_kernel(bins, docs, lengths, e, w, tokens, kv, qc, shared, acc, fetched, stats, sems):
    step = pl.program_id(0)

    def fetch(b):
        return pltpu.make_async_copy(tokens.at[bins[b], 128:384, :], fetched.at[b], sems.at[b])

    @pl.when(step == 0)
    def _():
        for b in range(EBLK):
            fetch(b).start()

    part = jnp.dot(e[...], w[...].reshape(-1, 2 * HD), preferred_element_type=f32)

    @pl.when(step == 0)
    def _():
        acc[...] = part

    @pl.when(step > 0)
    def _():
        acc[...] += part

    @pl.when(step == pl.num_programs(0) - 1)
    def _():
        kv[...] = acc[...].astype(bf16)
        stats[...] = jnp.zeros_like(stats)
        for b in range(EBLK):
            fetch(b).wait()
            first, _ = token_range(b, bins, docs, lengths)
            turned = pltpu.roll(fetched[b].astype(f32), lax.rem(2 * WIN - first, 2 * WIN), 0)
            qc[b] = turned[:WIN].astype(bf16)
        for b in range(EBLK):
            scores, raw, live = block_scores(b, bins, docs, lengths, kv, qc)
            scores = jnp.where(live, scores, MASKED)
            top = jnp.max(scores, axis=0, keepdims=True)
            raised = jnp.where(live, jnp.exp(scores - top), 0.0)
            stats[b : b + 1, :] = top
            stats[8 + b : 9 + b, :] = jnp.sum(raised, axis=0, keepdims=True)
            stats[16 + b : 17 + b, :] = jnp.sum(raised * raw, axis=0, keepdims=True)
        shared[...] = jnp.broadcast_to(stats[...][None], shared.shape)


def attend_kernel(bins, docs, lengths, kv, qc, stats, ids, grads, grads_t, slots, zero, made, sems):
    def copy(source, j):
        return pltpu.make_async_copy(source, slots.at[j], sems.at[j])

    zero[...] = jnp.zeros_like(zero)

    def clear(j, carry):
        used = bins[0] == j
        for b in range(1, EBLK):
            used = used | (bins[b] == j)

        @pl.when(jnp.logical_not(used))
        def _():
            copy(zero, j).start()

        return carry

    lax.fori_loop(0, BINS, clear, 0)

    tops = stats[:, 0:8, :].reshape(-1, WIN)
    sums = stats[:, 8:16, :].reshape(-1, WIN)
    dots = stats[:, 16:24, :].reshape(-1, WIN)
    owners = ids[...].reshape(-1, WIN)
    for b in range(EBLK):
        scores, raw, live = block_scores(b, bins, docs, lengths, kv, qc)
        same = owners == (bins[b] * NDOC + docs[b]).astype(f32)
        masked = jnp.where(same, tops, MASKED)
        top = jnp.max(masked, axis=0, keepdims=True)
        level = jnp.where(same, jnp.exp(masked - top), 0.0)
        total = jnp.maximum(jnp.sum(level * sums, axis=0, keepdims=True), 1.0)
        delta = jnp.sum(level * dots, axis=0, keepdims=True) / total
        attention = jnp.exp(jnp.where(live, scores - top, MASKED)) / total
        rounded = attention.astype(bf16)
        score_grad = (attention * (raw - delta) * SCALE).astype(bf16)
        rows = slice(b * BLK, (b + 1) * BLK)
        query, cotangent = qc[b, :, :HD], qc[b, :, HD:]
        made[b, :, :HD] = mul(rounded, kv[rows, HD:], 0, 0).astype(bf16)
        made[b, :, HD:] = mul(score_grad, kv[rows, :HD], 0, 0).astype(bf16)
        copy(made.at[b], bins[b]).start()
        grads[rows, :HD] = mul(score_grad, query, 1, 0).astype(bf16)
        grads[rows, HD:] = mul(rounded, cotangent, 1, 0).astype(bf16)
        grads_t[:HD, rows] = mul(query, score_grad, 0, 1).astype(bf16)
        grads_t[HD:, rows] = mul(cotangent, rounded, 0, 1).astype(bf16)

    def finish(j, carry):
        copy(zero, j).wait()
        return carry

    lax.fori_loop(0, BINS, finish, 0)


def collect_kernel(docs, lengths, windows, context, query_grad, acc):
    step = pl.program_id(0)

    @pl.when(step == 0)
    def _():
        acc[...] = jnp.zeros_like(acc)

    for i in range(windows.shape[0]):
        acc[docs[step * windows.shape[0] + i]] += windows[i].astype(f32)

    @pl.when(step == pl.num_programs(0) - 1)
    def _():
        total = jnp.concatenate([acc[0], jnp.zeros_like(acc[0])], axis=0)
        first = lengths[0, 0]
        for k in range(1, NDOC):
            total += pltpu.roll(jnp.concatenate([acc[k], jnp.zeros_like(acc[k])], axis=0), first, 0)
            first = first + lengths[0, k]
        context[...] = total[:, :HD].astype(bf16)
        query_grad[...] = total[:, HD:].astype(bf16)


def rows_kernel(grads, w, out):
    terms = mul(grads[...], w[...].reshape(-1, 2 * HD), 1, 1).astype(bf16)
    for i in range(out.shape[0]):
        out[i] = terms[:, i * 512 : (i + 1) * 512]


def weights_kernel(grads_t, e, mine, other):
    core = lax.axis_index("c")
    term = jnp.dot(grads_t[...], e[...], preferred_element_type=f32).astype(bf16)
    for i in range(term.shape[1] // 256):
        even, odd = term[:, i * 256 : i * 256 + 128], term[:, i * 256 + 128 : i * 256 + 256]
        mine[i] = jnp.where(core == 0, even, odd)
        other[i] = jnp.where(core == 0, odd, even)


def turn_kernel(weights, key, value):
    key[...] = weights[:HD].astype(f32).T.astype(bf16)
    value[...] = weights[HD:].astype(f32).T.astype(bf16)


def shape(*dims, dtype=bf16):
    return jax.ShapeDtypeStruct(dims, dtype)


def send(v, axis, distance):
    return lax.ppermute(v, axis, [(i, (i + distance) % 4) for i in range(4)])


def quarter_sum(terms, axis, dim):
    me = lax.axis_index(axis)

    def part(distance):
        return lax.dynamic_index_in_dim(terms, lax.rem(me + distance + 4, 4), dim, keepdims=False)

    far = part(2)
    half = far.shape[-2] // 2
    near = send(part(1), axis, 1), send(part(-1), axis, -1)
    top, low = send(far[..., :half, :], axis, 2), send(far[..., half:, :], axis, -2)
    total = part(0).astype(f32) + near[0].astype(f32) + near[1].astype(f32)
    return (total + jnp.concatenate([top, low], axis=-2).astype(f32)).astype(bf16)


def per_device(queries, context_grad, encoder_rows, key_weight, value_weight, document_lengths, block_bin, block_document):
    rows, width = encoder_rows.shape
    tokens = queries.shape[0]
    packed = jnp.concatenate(
        [
            jnp.concatenate([key_weight, value_weight], axis=1),
            jnp.concatenate([queries, context_grad], axis=1),
        ],
        axis=0,
    )
    gathered = lax.all_gather(packed, DP, axis=0, tiled=False)

    def share(v):
        spread_out = jnp.broadcast_to(v[None], (BINS, *v.shape))
        return lax.all_to_all(spread_out, DP, split_axis=0, concat_axis=0, tiled=True)

    facts = jnp.concatenate([document_lengths[0], block_bin * NDOC + block_document, jnp.full((1,), -1, jnp.int32)])
    facts = share(facts[None, :])[:, 0, :]
    lengths = facts[:, :NDOC]
    ids = jnp.broadcast_to(facts[:, NDOC:, None].astype(f32), (BINS, 8, WIN))
    sent = facts[:, NDOC : NDOC + EBLK]
    me = lax.axis_index(DP)
    sent_docs = jnp.sum(jnp.where(sent // NDOC == me, sent % NDOC, 0), axis=1)
    ids, sent_docs, lengths, gathered = lax.optimization_barrier((ids, sent_docs, lengths, gathered))

    kv, qc, stats = pl.pallas_call(
        project_kernel,
        grid=(4,),
        in_specs=[
            SMEM,
            SMEM,
            SMEM,
            pl.BlockSpec((rows, 1024), lambda k: (0, k)),
            pl.BlockSpec((8, 128, 2 * HD), lambda k: (k, 0, 0)),
            ANY,
        ],
        out_specs=[
            pl.BlockSpec((rows, 2 * HD), lambda k: (0, 0)),
            pl.BlockSpec((EBLK, WIN, 2 * HD), lambda k: (0, 0, 0)),
            pl.BlockSpec((BINS, 24, WIN), lambda k: (0, 0, 0)),
        ],
        out_shape=[shape(rows, 2 * HD), shape(EBLK, WIN, 2 * HD), shape(BINS, 24, WIN, dtype=f32)],
        scratch_shapes=[
            pltpu.VMEM((rows, 2 * HD), f32),
            pltpu.VMEM((EBLK, tokens, 2 * HD), bf16),
            pltpu.VMEM((24, WIN), f32),
            pltpu.SemaphoreType.DMA((EBLK,)),
        ],
        compiler_params=params(),
        name="project",
    )(block_bin, block_document, lengths, encoder_rows, gathered, gathered)

    all_stats = lax.all_to_all(stats, DP, split_axis=0, concat_axis=0, tiled=True)

    grads, grads_t, slots = pl.pallas_call(
        attend_kernel,
        in_specs=[SMEM, SMEM, SMEM, VMEM, VMEM, VMEM, VMEM],
        out_specs=[VMEM, VMEM, ANY],
        out_shape=[
            shape(rows, 2 * HD),
            shape(2 * HD, rows),
            shape(BINS, WIN, 2 * HD),
        ],
        scratch_shapes=[
            pltpu.VMEM((WIN, 2 * HD), bf16),
            pltpu.VMEM((EBLK, WIN, 2 * HD), bf16),
            pltpu.SemaphoreType.DMA((BINS,)),
        ],
        compiler_params=params(),
        name="attend",
    )(block_bin, block_document, lengths, kv, qc, all_stats, ids)

    windows = lax.all_to_all(slots, DP, split_axis=0, concat_axis=0, tiled=True)

    row_terms = pl.pallas_call(
        rows_kernel,
        grid=(4,),
        in_specs=[
            pl.BlockSpec((rows, 2 * HD), lambda k: (0, 0)),
            pl.BlockSpec((8, 128, 2 * HD), lambda k: (k, 0, 0)),
        ],
        out_specs=pl.BlockSpec((2, rows, 512), lambda k: (k, 0, 0)),
        out_shape=shape(8, rows, 512),
        compiler_params=params(),
        cost_estimate=COST,
        name="row_terms",
    )(grads, gathered)
    encoder_grad = lax.psum_scatter(row_terms, "mp", scatter_dimension=0, tiled=False)


    mine_w, other_w = pl.pallas_call(
        weights_kernel,
        grid=(4,),
        in_specs=[
            pl.BlockSpec((2 * HD, rows), lambda k: (0, 0)),
            pl.BlockSpec((rows, 1024), lambda k: (0, k)),
        ],
        out_specs=[pl.BlockSpec((4, 2 * HD, 128), lambda k: (k, 0, 0))] * 2,
        out_shape=[shape(16, 2 * HD, 128)] * 2,
        compiler_params=params(),
        cost_estimate=COST,
        name="weight_terms",
    )(grads_t, encoder_rows)
    arrived = lax.ppermute(other_w, "c", [(0, 1), (1, 0)])
    pair_sums = (mine_w.astype(f32) + arrived.astype(f32)).astype(bf16)
    weights = quarter_sum(pair_sums.reshape(4, 4, 2 * HD, 128), "x", 1)
    weights = quarter_sum(weights, "y", 0)
    key_weight_grad, value_weight_grad = pl.pallas_call(
        turn_kernel,
        in_specs=[VMEM],
        out_specs=[VMEM] * 2,
        out_shape=[shape(128, HD)] * 2,
        name="turn",
    )(weights)

    context, query_grad = pl.pallas_call(
        collect_kernel,
        grid=(8,),
        in_specs=[SMEM, SMEM, pl.BlockSpec((4, WIN, 2 * HD), lambda k: (k, 0, 0))],
        out_specs=[pl.BlockSpec((tokens, HD), lambda k: (0, 0))] * 2,
        out_shape=[shape(tokens, HD)] * 2,
        scratch_shapes=[pltpu.VMEM((NDOC, WIN, 2 * HD), f32)],
        compiler_params=params(),
        name="collect",
    )(sent_docs, document_lengths, windows)

    return context, query_grad, encoder_grad, key_weight_grad, value_weight_grad


def solution(mesh):
    fine = Mesh(mesh.devices.reshape(4, 4, 2, 8), ("y", "x", "c", "mp"))
    both, first = P(DP, "mp"), P(DP)
    return jax.shard_map(
        per_device,
        mesh=fine,
        in_specs=(both, both, P(DP, None), both, both, P(DP, None), first, first),
        out_specs=(both,) * 5,
        check_vma=False,
    )
```

```python
import jax
import jax.numpy as jnp
from jax import lax
from jax.experimental import pallas as pl
from jax.experimental.pallas import tpu as pltpu
from jax.sharding import Mesh
from jax.sharding import PartitionSpec as P

HD = 256
BLK = 128
EBLK = 7
NDOC = 4
WIN = 128
BINS = 32
MASKED = -1e30
SCALE = HD ** (-0.5)
PLANE = ("y", "x")
DP = ("y", "x", "c")
bf16, f32 = jnp.bfloat16, jnp.float32
VMEM = pl.BlockSpec(memory_space=pltpu.VMEM)
SMEM = pl.BlockSpec(memory_space=pltpu.SMEM)
COST = pl.CostEstimate(flops=3758096384, bytes_accessed=16 * 2**20, transcendentals=0)
ANY = pl.BlockSpec(memory_space=pl.ANY)


def mul(a, b, da, db):
    return lax.dot_general(a, b, (((da,), (db,)), ((), ())), preferred_element_type=f32)


def params(**more):
    return pltpu.CompilerParams(vmem_limit_bytes=56 * 2**20, **more)


def token_range(b, bins, docs, lengths):
    j, k = bins[b], docs[b]
    first = jnp.int32(0)
    for i in range(NDOC - 1):
        first = first + jnp.where(i < k, lengths[j, i], 0)
    return first, first + lengths[j, k]


def block_scores(b, bins, docs, lengths, kv, qc):
    first, last = token_range(b, bins, docs, lengths)
    key, value = kv[b * BLK : (b + 1) * BLK, :HD], kv[b * BLK : (b + 1) * BLK, HD:]
    scores = mul(key, qc[b, :, :HD], 1, 1) * SCALE
    raw = mul(value, qc[b, :, HD:], 1, 1)
    return scores, raw, lax.broadcasted_iota(jnp.int32, scores.shape, 1) < last - first


def project_kernel(bins, docs, lengths, e, w, near, far, kv, qc, shared, acc, fetched, stats, sems):
    step = pl.program_id(0)

    core = lax.axis_index("c")

    def fetch(b, held, do):
        j = bins[b]
        back_x = lax.rem(lax.axis_index("x") + 4 - lax.rem(lax.div(j, 2), 4), 4)
        back_y = lax.rem(lax.axis_index("y") + 4 - lax.div(j, 8), 4)
        do(pltpu.make_async_copy(held.at[0, back_x, back_y], fetched.at[b, :WIN, :], sems.at[b, 0]))
        do(pltpu.make_async_copy(held.at[1, back_y, back_x], fetched.at[b, WIN:, :], sems.at[b, 1]))

    @pl.when(step == 0)
    def _():
        for b in range(EBLK):

            @pl.when(lax.rem(bins[b], 2) == core)
            def _():
                fetch(b, near, lambda copy: copy.start())

            @pl.when(lax.rem(bins[b], 2) != core)
            def _():
                fetch(b, far, lambda copy: copy.start())

    part = jnp.dot(e[...], w[...].reshape(-1, 2 * HD), preferred_element_type=f32)

    @pl.when(step == 0)
    def _():
        acc[...] = part

    @pl.when(step > 0)
    def _():
        acc[...] += part

    @pl.when(step == pl.num_programs(0) - 1)
    def _():
        kv[...] = acc[...].astype(bf16)
        stats[...] = jnp.zeros_like(stats)
        for b in range(EBLK):
            fetch(b, near, lambda copy: copy.wait())
            first, _ = token_range(b, bins, docs, lengths)
            turned = pltpu.roll(fetched[b].astype(f32), lax.rem(2 * WIN - first, 2 * WIN), 0)
            qc[b] = turned[:WIN].astype(bf16)
        for b in range(EBLK):
            scores, raw, live = block_scores(b, bins, docs, lengths, kv, qc)
            scores = jnp.where(live, scores, MASKED)
            top = jnp.max(scores, axis=0, keepdims=True)
            raised = jnp.where(live, jnp.exp(scores - top), 0.0)
            stats[b : b + 1, :] = top
            stats[8 + b : 9 + b, :] = jnp.sum(raised, axis=0, keepdims=True)
            stats[16 + b : 17 + b, :] = jnp.sum(raised * raw, axis=0, keepdims=True)
        shared[...] = jnp.broadcast_to(stats[...][None], shared.shape)


def attend_kernel(bins, docs, lengths, kv, qc, stats, ids, grads, grads_t, slots, zero, made, sems):
    def copy(source, j):
        return pltpu.make_async_copy(source, slots.at[j], sems.at[j])

    zero[...] = jnp.zeros_like(zero)

    def clear(j, carry):
        used = bins[0] == j
        for b in range(1, EBLK):
            used = used | (bins[b] == j)

        @pl.when(jnp.logical_not(used))
        def _():
            copy(zero, j).start()

        return carry

    lax.fori_loop(0, BINS, clear, 0)

    tops = stats[:, 0:8, :].reshape(-1, WIN)
    sums = stats[:, 8:16, :].reshape(-1, WIN)
    dots = stats[:, 16:24, :].reshape(-1, WIN)
    owners = ids[...].reshape(-1, WIN)
    for b in range(EBLK):
        scores, raw, live = block_scores(b, bins, docs, lengths, kv, qc)
        same = owners == (bins[b] * NDOC + docs[b]).astype(f32)
        masked = jnp.where(same, tops, MASKED)
        top = jnp.max(masked, axis=0, keepdims=True)
        level = jnp.where(same, jnp.exp(masked - top), 0.0)
        total = jnp.maximum(jnp.sum(level * sums, axis=0, keepdims=True), 1.0)
        delta = jnp.sum(level * dots, axis=0, keepdims=True) / total
        attention = jnp.exp(jnp.where(live, scores - top, MASKED)) / total
        rounded = attention.astype(bf16)
        score_grad = (attention * (raw - delta) * SCALE).astype(bf16)
        rows = slice(b * BLK, (b + 1) * BLK)
        query, cotangent = qc[b, :, :HD], qc[b, :, HD:]
        made[b, :, :HD] = mul(rounded, kv[rows, HD:], 0, 0).astype(bf16)
        made[b, :, HD:] = mul(score_grad, kv[rows, :HD], 0, 0).astype(bf16)
        copy(made.at[b], bins[b]).start()
        grads[rows, :HD] = mul(score_grad, query, 1, 0).astype(bf16)
        grads[rows, HD:] = mul(rounded, cotangent, 1, 0).astype(bf16)
        grads_t[:HD, rows] = mul(query, score_grad, 0, 1).astype(bf16)
        grads_t[HD:, rows] = mul(cotangent, rounded, 0, 1).astype(bf16)

    def finish(j, carry):
        copy(zero, j).wait()
        return carry

    lax.fori_loop(0, BINS, finish, 0)


def collect_kernel(docs, lengths, windows, context, query_grad, acc):
    step = pl.program_id(0)

    @pl.when(step == 0)
    def _():
        acc[...] = jnp.zeros_like(acc)

    for i in range(windows.shape[0]):
        acc[docs[step * windows.shape[0] + i]] += windows[i].astype(f32)

    @pl.when(step == pl.num_programs(0) - 1)
    def _():
        total = jnp.concatenate([acc[0], jnp.zeros_like(acc[0])], axis=0)
        first = lengths[0, 0]
        for k in range(1, NDOC):
            total += pltpu.roll(jnp.concatenate([acc[k], jnp.zeros_like(acc[k])], axis=0), first, 0)
            first = first + lengths[0, k]
        context[...] = total[:, :HD].astype(bf16)
        query_grad[...] = total[:, HD:].astype(bf16)


def rows_kernel(grads, w, out):
    terms = mul(grads[...], w[...].reshape(-1, 2 * HD), 1, 1).astype(bf16)
    for i in range(out.shape[0]):
        out[i] = terms[:, i * 512 : (i + 1) * 512]


def weights_kernel(grads_t, e, mine, other):
    core = lax.axis_index("c")
    term = jnp.dot(grads_t[...], e[...], preferred_element_type=f32).astype(bf16)
    for i in range(term.shape[1] // 256):
        even, odd = term[:, i * 256 : i * 256 + 128], term[:, i * 256 + 128 : i * 256 + 256]
        mine[i] = jnp.where(core == 0, even, odd)
        other[i] = jnp.where(core == 0, odd, even)


def shape(*dims, dtype=bf16):
    return jax.ShapeDtypeStruct(dims, dtype)


def gather_ring(v, axis):
    def send(part, distance):
        return lax.ppermute(part, axis, [(i, (i + distance) % 4) for i in range(4)])

    half = v.shape[-2] // 2
    across = jnp.concatenate([send(v[..., :half, :], 2), send(v[..., half:, :], -2)], axis=-2)
    return jnp.stack([v, send(v, 1), across, send(v, -1)])


def per_device(queries, context_grad, encoder_rows, key_weight, value_weight, document_lengths, block_bin, block_document):
    rows, width = encoder_rows.shape
    tokens = queries.shape[0]
    gathered = lax.all_gather(jnp.concatenate([key_weight, value_weight], axis=1), DP, axis=0, tiled=False)
    own_tokens = jnp.concatenate([queries, context_grad], axis=1)
    near_tokens = jnp.stack(
        [
            gather_ring(gather_ring(own_tokens[:WIN], "y"), "x"),
            gather_ring(gather_ring(own_tokens[WIN:], "x"), "y"),
        ]
    )
    far_tokens = lax.ppermute(near_tokens, "c", [(0, 1), (1, 0)])

    def share(v):
        spread_out = jnp.broadcast_to(v[None], (BINS, *v.shape))
        return lax.all_to_all(spread_out, DP, split_axis=0, concat_axis=0, tiled=True)

    facts = jnp.concatenate([document_lengths[0], block_bin * NDOC + block_document, jnp.full((1,), -1, jnp.int32)])
    facts = share(facts[None, :])[:, 0, :]
    lengths = facts[:, :NDOC]
    ids = jnp.broadcast_to(facts[:, NDOC:, None].astype(f32), (BINS, 8, WIN))
    sent = facts[:, NDOC : NDOC + EBLK]
    me = lax.axis_index(DP)
    sent_docs = jnp.sum(jnp.where(sent // NDOC == me, sent % NDOC, 0), axis=1)
    ids, sent_docs, lengths, gathered = lax.optimization_barrier((ids, sent_docs, lengths, gathered))

    kv, qc, stats = pl.pallas_call(
        project_kernel,
        grid=(4,),
        in_specs=[
            SMEM,
            SMEM,
            SMEM,
            pl.BlockSpec((rows, 1024), lambda k: (0, k)),
            pl.BlockSpec((8, 128, 2 * HD), lambda k: (k, 0, 0)),
            ANY,
            ANY,
        ],
        out_specs=[
            pl.BlockSpec((rows, 2 * HD), lambda k: (0, 0)),
            pl.BlockSpec((EBLK, WIN, 2 * HD), lambda k: (0, 0, 0)),
            pl.BlockSpec((BINS, 24, WIN), lambda k: (0, 0, 0)),
        ],
        out_shape=[shape(rows, 2 * HD), shape(EBLK, WIN, 2 * HD), shape(BINS, 24, WIN, dtype=f32)],
        scratch_shapes=[
            pltpu.VMEM((rows, 2 * HD), f32),
            pltpu.VMEM((EBLK, tokens, 2 * HD), bf16),
            pltpu.VMEM((24, WIN), f32),
            pltpu.SemaphoreType.DMA((EBLK, 2)),
        ],
        compiler_params=params(),
        name="project",
    )(block_bin, block_document, lengths, encoder_rows, gathered, near_tokens, far_tokens)

    all_stats = lax.all_to_all(stats, DP, split_axis=0, concat_axis=0, tiled=True)

    grads, grads_t, slots = pl.pallas_call(
        attend_kernel,
        in_specs=[SMEM, SMEM, SMEM, VMEM, VMEM, VMEM, VMEM],
        out_specs=[VMEM, VMEM, ANY],
        out_shape=[
            shape(rows, 2 * HD),
            shape(2 * HD, rows),
            shape(BINS, WIN, 2 * HD),
        ],
        scratch_shapes=[
            pltpu.VMEM((WIN, 2 * HD), bf16),
            pltpu.VMEM((EBLK, WIN, 2 * HD), bf16),
            pltpu.SemaphoreType.DMA((BINS,)),
        ],
        compiler_params=params(),
        name="attend",
    )(block_bin, block_document, lengths, kv, qc, all_stats, ids)

    windows = lax.all_to_all(slots, DP, split_axis=0, concat_axis=0, tiled=True)

    row_terms = pl.pallas_call(
        rows_kernel,
        grid=(4,),
        in_specs=[
            pl.BlockSpec((rows, 2 * HD), lambda k: (0, 0)),
            pl.BlockSpec((8, 128, 2 * HD), lambda k: (k, 0, 0)),
        ],
        out_specs=pl.BlockSpec((2, rows, 512), lambda k: (k, 0, 0)),
        out_shape=shape(8, rows, 512),
        compiler_params=params(),
        cost_estimate=COST,
        name="row_terms",
    )(grads, gathered)
    encoder_grad = lax.psum_scatter(row_terms, "mp", scatter_dimension=0, tiled=False)


    mine_w, other_w = pl.pallas_call(
        weights_kernel,
        grid=(4,),
        in_specs=[
            pl.BlockSpec((2 * HD, rows), lambda k: (0, 0)),
            pl.BlockSpec((rows, 1024), lambda k: (0, k)),
        ],
        out_specs=[pl.BlockSpec((4, 2 * HD, 128), lambda k: (k, 0, 0))] * 2,
        out_shape=[shape(16, 2 * HD, 128)] * 2,
        compiler_params=params(),
        cost_estimate=COST,
        name="weight_terms",
    )(grads_t, encoder_rows)
    arrived = lax.ppermute(other_w, "c", [(0, 1), (1, 0)])
    pair_sums = (mine_w.astype(f32) + arrived.astype(f32)).astype(bf16)
    windows, pair_sums = lax.optimization_barrier((windows, pair_sums))
    weight_sums = lax.all_to_all(pair_sums, PLANE, split_axis=0, concat_axis=0, tiled=True)

    context, query_grad = pl.pallas_call(
        collect_kernel,
        grid=(8,),
        in_specs=[SMEM, SMEM, pl.BlockSpec((4, WIN, 2 * HD), lambda k: (k, 0, 0))],
        out_specs=[pl.BlockSpec((tokens, HD), lambda k: (0, 0))] * 2,
        out_shape=[shape(tokens, HD)] * 2,
        scratch_shapes=[pltpu.VMEM((NDOC, WIN, 2 * HD), f32)],
        compiler_params=params(),
        name="collect",
    )(sent_docs, document_lengths, windows)

    weights = jnp.sum(weight_sums.astype(f32), axis=0).astype(bf16).T
    return context, query_grad, encoder_grad, weights[:, :HD], weights[:, HD:]


def solution(mesh):
    fine = Mesh(mesh.devices.reshape(4, 4, 2, 8), ("y", "x", "c", "mp"))
    both, first = P(DP, "mp"), P(DP)
    return jax.shard_map(
        per_device,
        mesh=fine,
        in_specs=(both, both, P(DP, None), both, both, P(DP, None), first, first),
        out_specs=(both,) * 5,
        check_vma=False,
    )
```

```python
import jax
import jax.numpy as jnp
from jax import lax
from jax.experimental import pallas as pl
from jax.experimental.pallas import tpu as pltpu
from jax.sharding import Mesh
from jax.sharding import PartitionSpec as P

HD = 256
BLK = 128
EBLK = 7
NDOC = 4
WIN = 128
BINS = 32
MASKED = -1e30
SCALE = HD ** (-0.5)
PLANE = ("y", "x")
DP = ("y", "x", "c")
bf16, f32 = jnp.bfloat16, jnp.float32
VMEM = pl.BlockSpec(memory_space=pltpu.VMEM)
SMEM = pl.BlockSpec(memory_space=pltpu.SMEM)
COST = pl.CostEstimate(flops=3758096384, bytes_accessed=16 * 2**20, transcendentals=0)
ANY = pl.BlockSpec(memory_space=pl.ANY)


def mul(a, b, da, db):
    return lax.dot_general(a, b, (((da,), (db,)), ((), ())), preferred_element_type=f32)


def params(**more):
    return pltpu.CompilerParams(vmem_limit_bytes=56 * 2**20, **more)


def token_range(b, bins, docs, lengths):
    j, k = bins[b], docs[b]
    first = jnp.int32(0)
    for i in range(NDOC - 1):
        first = first + jnp.where(i < k, lengths[j, i], 0)
    return first, first + lengths[j, k]


def block_scores(b, bins, docs, lengths, kv, qc):
    first, last = token_range(b, bins, docs, lengths)
    key, value = kv[b * BLK : (b + 1) * BLK, :HD], kv[b * BLK : (b + 1) * BLK, HD:]
    scores = mul(key, qc[b, :, :HD], 1, 1) * SCALE
    raw = mul(value, qc[b, :, HD:], 1, 1)
    return scores, raw, lax.broadcasted_iota(jnp.int32, scores.shape, 1) < last - first


def project_kernel(bins, docs, lengths, e, w, near, far, kv, qc, shared, acc, fetched, stats, sems):
    step = pl.program_id(0)

    core = lax.axis_index("c")

    def fetch(b, held, do):
        j = bins[b]
        back_x = lax.rem(lax.axis_index("x") + 4 - lax.rem(lax.div(j, 2), 4), 4)
        back_y = lax.rem(lax.axis_index("y") + 4 - lax.div(j, 8), 4)
        do(pltpu.make_async_copy(held.at[0, back_x, back_y], fetched.at[b, :WIN, :], sems.at[b, 0]))
        do(pltpu.make_async_copy(held.at[1, back_y, back_x], fetched.at[b, WIN:, :], sems.at[b, 1]))

    @pl.when(step == 0)
    def _():
        for b in range(EBLK):

            @pl.when(lax.rem(bins[b], 2) == core)
            def _():
                fetch(b, near, lambda copy: copy.start())

            @pl.when(lax.rem(bins[b], 2) != core)
            def _():
                fetch(b, far, lambda copy: copy.start())

    part = jnp.dot(e[...], w[...].reshape(-1, 2 * HD), preferred_element_type=f32)

    @pl.when(step == 0)
    def _():
        acc[...] = part

    @pl.when(step > 0)
    def _():
        acc[...] += part

    @pl.when(step == pl.num_programs(0) - 1)
    def _():
        kv[...] = acc[...].astype(bf16)
        stats[...] = jnp.zeros_like(stats)
        for b in range(EBLK):
            fetch(b, near, lambda copy: copy.wait())
            first, _ = token_range(b, bins, docs, lengths)
            turned = pltpu.roll(fetched[b].astype(f32), lax.rem(2 * WIN - first, 2 * WIN), 0)
            qc[b] = turned[:WIN].astype(bf16)
        for b in range(EBLK):
            scores, raw, live = block_scores(b, bins, docs, lengths, kv, qc)
            scores = jnp.where(live, scores, MASKED)
            top = jnp.max(scores, axis=0, keepdims=True)
            raised = jnp.where(live, jnp.exp(scores - top), 0.0)
            stats[b : b + 1, :] = top
            stats[8 + b : 9 + b, :] = jnp.sum(raised, axis=0, keepdims=True)
            stats[16 + b : 17 + b, :] = jnp.sum(raised * raw, axis=0, keepdims=True)
        shared[...] = jnp.broadcast_to(stats[...][None], shared.shape)


def attend_kernel(bins, docs, lengths, kv, qc, stats, ids, grads, grads_t, slots, zero, made, sems):
    def copy(source, j):
        return pltpu.make_async_copy(source, slots.at[j], sems.at[j])

    zero[...] = jnp.zeros_like(zero)

    def clear(j, carry):
        used = bins[0] == j
        for b in range(1, EBLK):
            used = used | (bins[b] == j)

        @pl.when(jnp.logical_not(used))
        def _():
            copy(zero, j).start()

        return carry

    lax.fori_loop(0, BINS, clear, 0)

    tops = stats[:, 0:8, :].reshape(-1, WIN)
    sums = stats[:, 8:16, :].reshape(-1, WIN)
    dots = stats[:, 16:24, :].reshape(-1, WIN)
    owners = ids[...].reshape(-1, WIN)
    for b in range(EBLK):
        scores, raw, live = block_scores(b, bins, docs, lengths, kv, qc)
        same = owners == (bins[b] * NDOC + docs[b]).astype(f32)
        masked = jnp.where(same, tops, MASKED)
        top = jnp.max(masked, axis=0, keepdims=True)
        level = jnp.where(same, jnp.exp(masked - top), 0.0)
        total = jnp.maximum(jnp.sum(level * sums, axis=0, keepdims=True), 1.0)
        delta = jnp.sum(level * dots, axis=0, keepdims=True) / total
        attention = jnp.exp(jnp.where(live, scores - top, MASKED)) / total
        rounded = attention.astype(bf16)
        score_grad = (attention * (raw - delta) * SCALE).astype(bf16)
        rows = slice(b * BLK, (b + 1) * BLK)
        query, cotangent = qc[b, :, :HD], qc[b, :, HD:]
        made[b, :, :HD] = mul(rounded, kv[rows, HD:], 0, 0).astype(bf16)
        made[b, :, HD:] = mul(score_grad, kv[rows, :HD], 0, 0).astype(bf16)
        copy(made.at[b], bins[b]).start()
        grads[rows, :HD] = mul(score_grad, query, 1, 0).astype(bf16)
        grads[rows, HD:] = mul(rounded, cotangent, 1, 0).astype(bf16)
        grads_t[:HD, rows] = mul(query, score_grad, 0, 1).astype(bf16)
        grads_t[HD:, rows] = mul(cotangent, rounded, 0, 1).astype(bf16)

    def finish(j, carry):
        copy(zero, j).wait()
        return carry

    lax.fori_loop(0, BINS, finish, 0)


def collect_kernel(docs, lengths, windows, context, query_grad, acc):
    step = pl.program_id(0)

    @pl.when(step == 0)
    def _():
        acc[...] = jnp.zeros_like(acc)

    for i in range(windows.shape[0]):
        acc[docs[step * windows.shape[0] + i]] += windows[i].astype(f32)

    @pl.when(step == pl.num_programs(0) - 1)
    def _():
        total = jnp.concatenate([acc[0], jnp.zeros_like(acc[0])], axis=0)
        first = lengths[0, 0]
        for k in range(1, NDOC):
            total += pltpu.roll(jnp.concatenate([acc[k], jnp.zeros_like(acc[k])], axis=0), first, 0)
            first = first + lengths[0, k]
        context[...] = total[:, :HD].astype(bf16)
        query_grad[...] = total[:, HD:].astype(bf16)


def rows_kernel(grads, w, out):
    terms = mul(grads[...], w[...].reshape(-1, 2 * HD), 1, 1).astype(bf16)
    for i in range(out.shape[0]):
        out[i] = terms[:, i * 512 : (i + 1) * 512]


def weights_kernel(grads_t, e, mine, other):
    core = lax.axis_index("c")
    term = jnp.dot(grads_t[...], e[...], preferred_element_type=f32).astype(bf16)
    for i in range(term.shape[1] // 256):
        even, odd = term[:, i * 256 : i * 256 + 128], term[:, i * 256 + 128 : i * 256 + 256]
        mine[i] = jnp.where(core == 0, even, odd)
        other[i] = jnp.where(core == 0, odd, even)


def shape(*dims, dtype=bf16):
    return jax.ShapeDtypeStruct(dims, dtype)


def gather_ring(v, axis):
    def send(part, distance):
        return lax.ppermute(part, axis, [(i, (i + distance) % 4) for i in range(4)])

    half = v.shape[-2] // 2
    across = jnp.concatenate([send(v[..., :half, :], 2), send(v[..., half:, :], -2)], axis=-2)
    return jnp.stack([v, send(v, 1), across, send(v, -1)])


def per_device(queries, context_grad, encoder_rows, key_weight, value_weight, document_lengths, block_bin, block_document):
    rows, width = encoder_rows.shape
    tokens = queries.shape[0]
    facts = jnp.concatenate([document_lengths[0], block_bin, block_document]).astype(bf16)
    packed = jnp.concatenate(
        [
            jnp.concatenate([key_weight, value_weight], axis=1),
            jnp.pad(facts[None, :], ((0, 15), (0, 2 * HD - facts.shape[0]))),
        ],
        axis=0,
    )
    gathered = lax.all_gather(packed, DP, axis=0, tiled=False)
    own_tokens = jnp.concatenate([queries, context_grad], axis=1)
    near_tokens = jnp.stack(
        [
            gather_ring(gather_ring(own_tokens[:WIN], "y"), "x"),
            gather_ring(gather_ring(own_tokens[WIN:], "x"), "y"),
        ]
    )
    far_tokens = lax.ppermute(near_tokens, "c", [(0, 1), (1, 0)])

    facts = gathered[:, BLK, : NDOC + 2 * EBLK].astype(jnp.int32)
    lengths, bins, docs = facts[:, :NDOC], facts[:, NDOC : NDOC + EBLK], facts[:, NDOC + EBLK :]
    ids = jnp.pad((bins * NDOC + docs).astype(f32), ((0, 0), (0, 1)), constant_values=-1.0)
    ids = jnp.broadcast_to(ids[:, :, None], (BINS, 8, WIN))
    sent_docs = jnp.sum(jnp.where(bins == lax.axis_index(DP), docs, 0), axis=1)
    ids, sent_docs, lengths = lax.optimization_barrier((ids, sent_docs, lengths))

    kv, qc, stats = pl.pallas_call(
        project_kernel,
        grid=(4,),
        in_specs=[
            SMEM,
            SMEM,
            SMEM,
            pl.BlockSpec((rows, 1024), lambda k: (0, k)),
            pl.BlockSpec((8, 128, 2 * HD), lambda k: (k, 0, 0)),
            ANY,
            ANY,
        ],
        out_specs=[
            pl.BlockSpec((rows, 2 * HD), lambda k: (0, 0)),
            pl.BlockSpec((EBLK, WIN, 2 * HD), lambda k: (0, 0, 0)),
            pl.BlockSpec((BINS, 24, WIN), lambda k: (0, 0, 0)),
        ],
        out_shape=[shape(rows, 2 * HD), shape(EBLK, WIN, 2 * HD), shape(BINS, 24, WIN, dtype=f32)],
        scratch_shapes=[
            pltpu.VMEM((rows, 2 * HD), f32),
            pltpu.VMEM((EBLK, tokens, 2 * HD), bf16),
            pltpu.VMEM((24, WIN), f32),
            pltpu.SemaphoreType.DMA((EBLK, 2)),
        ],
        compiler_params=params(),
        name="project",
    )(block_bin, block_document, lengths, encoder_rows, gathered, near_tokens, far_tokens)

    all_stats = lax.all_to_all(stats, DP, split_axis=0, concat_axis=0, tiled=True)

    grads, grads_t, slots = pl.pallas_call(
        attend_kernel,
        in_specs=[SMEM, SMEM, SMEM, VMEM, VMEM, VMEM, VMEM],
        out_specs=[VMEM, VMEM, ANY],
        out_shape=[
            shape(rows, 2 * HD),
            shape(2 * HD, rows),
            shape(BINS, WIN, 2 * HD),
        ],
        scratch_shapes=[
            pltpu.VMEM((WIN, 2 * HD), bf16),
            pltpu.VMEM((EBLK, WIN, 2 * HD), bf16),
            pltpu.SemaphoreType.DMA((BINS,)),
        ],
        compiler_params=params(),
        name="attend",
    )(block_bin, block_document, lengths, kv, qc, all_stats, ids)

    windows = lax.all_to_all(slots, DP, split_axis=0, concat_axis=0, tiled=True)

    row_terms = pl.pallas_call(
        rows_kernel,
        grid=(4,),
        in_specs=[
            pl.BlockSpec((rows, 2 * HD), lambda k: (0, 0)),
            pl.BlockSpec((8, 128, 2 * HD), lambda k: (k, 0, 0)),
        ],
        out_specs=pl.BlockSpec((2, rows, 512), lambda k: (k, 0, 0)),
        out_shape=shape(8, rows, 512),
        compiler_params=params(),
        cost_estimate=COST,
        name="row_terms",
    )(grads, gathered)
    encoder_grad = lax.psum_scatter(row_terms, "mp", scatter_dimension=0, tiled=False)


    mine_w, other_w = pl.pallas_call(
        weights_kernel,
        grid=(4,),
        in_specs=[
            pl.BlockSpec((2 * HD, rows), lambda k: (0, 0)),
            pl.BlockSpec((rows, 1024), lambda k: (0, k)),
        ],
        out_specs=[pl.BlockSpec((4, 2 * HD, 128), lambda k: (k, 0, 0))] * 2,
        out_shape=[shape(16, 2 * HD, 128)] * 2,
        compiler_params=params(),
        cost_estimate=COST,
        name="weight_terms",
    )(grads_t, encoder_rows)
    arrived = lax.ppermute(other_w, "c", [(0, 1), (1, 0)])
    pair_sums = (mine_w.astype(f32) + arrived.astype(f32)).astype(bf16)
    windows, pair_sums = lax.optimization_barrier((windows, pair_sums))
    weight_sums = lax.all_to_all(pair_sums, PLANE, split_axis=0, concat_axis=0, tiled=True)

    context, query_grad = pl.pallas_call(
        collect_kernel,
        grid=(8,),
        in_specs=[SMEM, SMEM, pl.BlockSpec((4, WIN, 2 * HD), lambda k: (k, 0, 0))],
        out_specs=[pl.BlockSpec((tokens, HD), lambda k: (0, 0))] * 2,
        out_shape=[shape(tokens, HD)] * 2,
        scratch_shapes=[pltpu.VMEM((NDOC, WIN, 2 * HD), f32)],
        compiler_params=params(),
        name="collect",
    )(sent_docs, document_lengths, windows)

    weights = jnp.sum(weight_sums.astype(f32), axis=0).astype(bf16).T
    return context, query_grad, encoder_grad, weights[:, :HD], weights[:, HD:]


def solution(mesh):
    fine = Mesh(mesh.devices.reshape(4, 4, 2, 8), ("y", "x", "c", "mp"))
    both, first = P(DP, "mp"), P(DP)
    return jax.shard_map(
        per_device,
        mesh=fine,
        in_specs=(both, both, P(DP, None), both, both, P(DP, None), first, first),
        out_specs=(both,) * 5,
        check_vma=False,
    )
```
